128 devices in a mesh: pp: 8 (over y, x_lo), ep: 16 (over x_hi, z, core).
Axes of the slice: x: 4 (x_hi: 2, x_lo: 2; x = x_hi * 2 + x_lo), y: 4, z: 4, core: 2. Of those that a mesh axis runs over, the one named last changes fastest.
Arguments:
- fwd_sent: bfloat16 [8, 2048, 7168], P('pp', 'ep'), may hold values from -40 to 40
- bwd_sent: bfloat16 [8, 2048, 7168], P('pp', 'ep'), may hold values from -12 to 12
- bwd_saved: bfloat16 [8, 2048, 7168], P('pp', 'ep'), may hold values from -40 to 40
- bwd_pre: bfloat16 [8, 2048, 2, 2048], P('pp', 'ep'), may hold values from -5 to 5
- fwd_route: int32 [8, 2048, 2], P('pp', 'ep'), may hold values from 0 to 3, all different within a row; in each aligned block of 128 rows (0 to 127, 128 to 255, ..., all dimensions but the last counted through in order) at most 72 rows name the same one
- bwd_route: int32 [8, 2048, 2], P('pp', 'ep'), may hold values from 0 to 3, all different within a row; in each aligned block of 128 rows (0 to 127, 128 to 255, ..., all dimensions but the last counted through in order) at most 72 rows name the same one
- fwd_gate: float32 [8, 2048, 2], P('pp', 'ep'), may hold values from 0.2 to 1
- bwd_gate: float32 [8, 2048, 2], P('pp', 'ep'), may hold values from 0.2 to 1
- gain: float32 [8, 7168], P('pp'), may hold values from 0.5 to 1.5
- w_in: bfloat16 [8, 28672, 2048], P('pp', 'ep'), may hold values from -0.0625 to 0.0625
- w_out: bfloat16 [8, 1024, 28672], P('pp', None, 'ep'), may hold values from -0.1875 to 0.1875
Outputs:
- fwd_out: bfloat16 [8, 2048, 7168], P('pp', 'ep')
- bwd_out: bfloat16 [8, 2048, 7168], P('pp', 'ep')
- gain_grad: float32 [8, 7168], P('pp')
The draws below stay inside these ranges and needn't reach their ends.
Inputs may be any that keep to these rules, and one draw needn't show every extreme that they name: `fwd_route`: each token's 2 ids differ. In the 128 rows of one device no expert is named more than 72 times, and in every draw some expert is named exactly 72 times by the rows of some device. `bwd_route`: as for fwd_route.
All inputs are finite; a program needn't handle non-finite values.
Results may differ from the reference program's by a relative error of at most 0.0071.
Values may be sent and summed in bfloat16 or wider, within the bound.
A program may use at most 192 MiB of HBM per device.

```python
import math
import jax
import jax.numpy as jnp
import numpy as np
from jax import lax

D = 7168
FF = 1024
EXPERTS = 4
TOP = 2
TOK_DEV = 128
CAP = 72
SECTIONS = 8
TOKENS = 2048
N_EP = 16


def scale_grid(key):
    row_key, column_key = jax.random.split(key)
    row_scale = jnp.exp(jax.random.uniform(row_key, (SECTIONS, TOKENS, 1), jnp.float32, math.log(0.5), math.log(5.0)))
    column_scale = jnp.exp(jax.random.uniform(column_key, (1, 1, D), jnp.float32, math.log(0.5), math.log(2.0)))
    return row_scale * column_scale


def draw_fwd_sent(key, part):
    key = jax.random.fold_in(key, 11)
    base_key, scale_key = jax.random.split(key)
    base_values = jax.random.truncated_normal(base_key, -4.0, 4.0, (SECTIONS, TOKENS, D), jnp.float32)
    return (base_values * scale_grid(scale_key)).astype(jnp.bfloat16)


def draw_bwd_saved(key, part):
    key = jax.random.fold_in(key, 13)
    base_key, scale_key = jax.random.split(key)
    base_values = jax.random.truncated_normal(base_key, -4.0, 4.0, (SECTIONS, TOKENS, D), jnp.float32)
    return (base_values * scale_grid(scale_key)).astype(jnp.bfloat16)


def draw_bwd_sent(key, part):
    key = jax.random.fold_in(key, 17)
    base_values = jax.random.truncated_normal(key, -4.0, 4.0, (SECTIONS, TOKENS, D), jnp.float32)
    rising = 1.0 + 2.0 * jnp.arange(TOKENS, dtype=jnp.float32) / (TOKENS - 1)
    return (base_values * rising[None, :, None]).astype(jnp.bfloat16)


def level_of(own_key, extent, cuts, low, high):
    def one(position, shards_of):
        steps = jax.random.uniform(jax.random.fold_in(jax.random.fold_in(own_key, 6), position), (shards_of,), jnp.float32, low / len(cuts), high / len(cuts))
        return jnp.repeat(jnp.exp(steps), extent[position] // shards_of).reshape((-1,) + (1,) * (len(extent) - position - 1))

    level = one(*cuts[0])
    for cut in cuts[1:]:
        level = level * one(*cut)
    return level


def assign_block(rng, own, number, rows, count, top, reach, skew):
    order = jax.random.permutation(rng, count)
    heavy_load, usual = portions_of(count, rows * top, reach, skew, True), portions_of(count, rows * top, reach, skew, False)
    places = jnp.arange(count)

    def named(lengths, rotation):
        used = int((lengths > 0).sum())
        fixed = max(1, used // 4)
        shifted = fixed + (places - fixed + rotation * (used - fixed)) % max(1, count - fixed)
        return jnp.zeros((count,), jnp.int32).at[order[jnp.where(places < fixed, places, shifted)]].set(jnp.asarray(lengths, jnp.int32))

    lengths = jnp.where(number % 4 == 0, named(heavy_load, number // 4), named(usual, number - number // 4 - 1))
    mixed = jax.random.permutation(jax.random.fold_in(own, 3), count)
    donor, taker = mixed[0:count // 2 * 2:2], mixed[1:count // 2 * 2:2]
    slack = jnp.minimum(lengths[donor] - 1, reach - lengths[taker]) // 2
    slack = jnp.where((donor == order[0]) | (taker == order[0]) | (lengths[taker] == 0), 0, jnp.maximum(slack, 0))
    shifted = jax.random.randint(jax.random.fold_in(own, 4), (count // 2,), 0, 1 << 20) % (slack + 1)
    lengths = lengths.at[donor].add(-shifted).at[taker].add(shifted)
    members = jnp.searchsorted(jnp.cumsum(lengths), jnp.arange(rows * top), side="right").astype(jnp.int32)
    grid = members.reshape(top, rows).T
    grid = grid[jax.random.permutation(jax.random.fold_in(own, 1), rows)]
    rotation = jax.random.randint(jax.random.fold_in(own, 2), (rows, 1), 0, top)
    return jnp.take_along_axis(grid, (jnp.arange(top)[None, :] + rotation) % top, axis=1)


def portions_of(count, total, most, skew, full):
    weights = [(1 << 20) // math.isqrt(rank ** skew) + 1 for rank in range(1, count + 1)]
    largest = most if full else min(most, max(-(-total // count), total * weights[0] // sum(weights)))
    least = 1 if total - largest >= count - 1 else 0
    given, spare = [largest] + [least] * (count - 1), total - largest - least * (count - 1)
    while spare > 0:
        candidates = [i for i in range(1, count) if given[i] < largest] or [i for i in range(1, count) if given[i] < most]
        pool, budget = sum([weights[i] for i in candidates]), spare
        for i in candidates:
            more = min(most - given[i], max(1, budget * weights[i] // pool), spare)
            given[i] = given[i] + more
            spare = spare - more
    return np.array(given)


def bell_draw(stream_key, dims, width, reach, cuts=(), kind=jnp.bfloat16):
    loudness = level_of(stream_key, dims, cuts, -0.22, 0.18) if cuts else 1.0
    drawn = jax.random.normal(stream_key, dims, jnp.float32) * width * loudness
    return jnp.minimum(jnp.maximum(drawn, -reach), reach).astype(kind)


def setup_inputs(seed: int = 0) -> dict:
    arg_keys = jax.random.split(jax.random.key(seed), 12)
    fwd_sent = draw_fwd_sent(jax.random.fold_in(arg_keys[11], 71), 0)
    bwd_sent = draw_bwd_sent(jax.random.fold_in(arg_keys[11], 71), 0)
    bwd_saved = draw_bwd_saved(jax.random.fold_in(arg_keys[11], 71), 0)
    bwd_pre = bell_draw(arg_keys[3], (SECTIONS, TOKENS, TOP, 2 * FF), 1.0, 5.0, ((0, 8), (1, 16)))
    fwd_route_keys = jax.random.split(jax.random.fold_in(arg_keys[4], 1), SECTIONS * TOKENS // TOK_DEV)
    fwd_route_turns = jax.random.permutation(jax.random.fold_in(arg_keys[4], 3), SECTIONS * TOKENS // TOK_DEV)
    fwd_route = jax.vmap(lambda own, number: assign_block(jax.random.fold_in(arg_keys[4], 2), own, number, TOK_DEV, EXPERTS, TOP, CAP, 2))(fwd_route_keys, fwd_route_turns).reshape((SECTIONS, TOKENS, TOP))
    bwd_route_keys = jax.random.split(jax.random.fold_in(arg_keys[5], 1), SECTIONS * TOKENS // TOK_DEV)
    bwd_route_turns = jax.random.permutation(jax.random.fold_in(arg_keys[5], 3), SECTIONS * TOKENS // TOK_DEV)
    bwd_route = jax.vmap(lambda own, number: assign_block(jax.random.fold_in(arg_keys[5], 2), own, number, TOK_DEV, EXPERTS, TOP, CAP, 2))(bwd_route_keys, bwd_route_turns).reshape((SECTIONS, TOKENS, TOP))
    fwd_gate = jnp.clip(0.2 + 0.8 * jax.random.uniform(arg_keys[6], (SECTIONS, TOKENS, TOP), jnp.float32) ** level_of(arg_keys[6], (SECTIONS, TOKENS, TOP), ((0, 8), (1, 16)), -0.2, 0.2), 0.2, 1.0)
    bwd_gate = jnp.clip(0.2 + 0.8 * jax.random.uniform(arg_keys[7], (SECTIONS, TOKENS, TOP), jnp.float32) ** level_of(arg_keys[7], (SECTIONS, TOKENS, TOP), ((0, 8), (1, 16)), -0.2, 0.2), 0.2, 1.0)
    gain = jnp.clip(0.5 + 1.0 * jax.random.uniform(arg_keys[8], (SECTIONS, D), jnp.float32) ** level_of(arg_keys[8], (SECTIONS, D), ((0, 8),), -0.2, 0.2), 0.5, 1.5)
    w_in = bell_draw(arg_keys[9], (SECTIONS, EXPERTS * D, 2 * FF), D ** -0.5, 0.0625, ((0, 8), (1, 16)))
    w_out = bell_draw(arg_keys[10], (SECTIONS, FF, EXPERTS * D), FF ** -0.5, 0.1875, ((0, 8), (2, 16)))
    return {"fwd_sent": fwd_sent, "bwd_sent": bwd_sent, "bwd_saved": bwd_saved, "bwd_pre": bwd_pre, "fwd_route": fwd_route, "bwd_route": bwd_route, "fwd_gate": fwd_gate, "bwd_gate": bwd_gate, "gain": gain, "w_in": w_in, "w_out": w_out}


epsilon = 1e-06

def slot_place(route_flat, expert_total, capacity):
    expert_ids = jnp.arange(expert_total, dtype=jnp.int32)
    one_hot = (route_flat[..., None] == expert_ids).astype(jnp.int32)
    earlier = jnp.cumsum(one_hot, axis=-2) - one_hot
    return route_flat * capacity + lax.optimization_barrier(jnp.sum(earlier * one_hot, axis=-1))

def rounded(values):
    return lax.optimization_barrier(values.astype(jnp.bfloat16)).astype(jnp.float32)

def pair_total(pieces):
    level_sums = [rounded(member) for member in pieces]
    while len(level_sums) > 1:
        merged = [level_sums[offset] + level_sums[offset + 1] for offset in range(0, len(level_sums), 2)]
        if len(merged) > 1:
            merged = [rounded(member) for member in merged]
        level_sums = merged
    return level_sums[0]

def section_step(packed):
    fwd_in, grad_in, saved_in, saved_pre, route_fwd, route_bwd, gate_fwd, gate_bwd, gain_row, weight_in, weight_out = packed
    groups = N_EP
    slices = N_EP // EXPERTS
    piece_width = D // slices
    rows_all = groups * TOK_DEV
    pair_count = rows_all * TOP
    contract = (((1,), (1,)), ((), ()))

    def pair_layout(routes):
        place = slot_place(routes.reshape(groups, TOK_DEV * TOP), EXPERTS, CAP)
        expert_of = place // CAP
        slot_of = place % CAP
        source = jnp.arange(groups, dtype=jnp.int32)[:, None]
        flat = ((expert_of * groups + source) * CAP + slot_of).reshape(-1).astype(jnp.int32)
        inverse = jnp.full((EXPERTS * groups * CAP,), pair_count, jnp.int32).at[flat].set(jnp.arange(pair_count, dtype=jnp.int32))
        return (flat, inverse)

    def dispatch(pair_rows, inverse):
        padded = jnp.concatenate([pair_rows, jnp.zeros((1, pair_rows.shape[1]), pair_rows.dtype)], axis=0)
        return padded[inverse].reshape(EXPERTS, groups * CAP, pair_rows.shape[1])
    values = fwd_in.astype(jnp.float32)
    inv_rms = lax.rsqrt(lax.optimization_barrier(jnp.mean(values * values, axis=-1, keepdims=True)) + epsilon)
    normed = (values * inv_rms * gain_row).astype(jnp.bfloat16)
    flat_fwd, inverse_fwd = pair_layout(route_fwd)
    expert_rows = dispatch(jnp.repeat(normed, TOP, axis=0), inverse_fwd)
    outputs = []
    for expert in range(EXPERTS):
        rows_now = expert_rows[expert]
        base_row = expert * D
        pre_vals = pair_total([jnp.dot(rows_now[:, column * piece_width:(column + 1) * piece_width], weight_in[base_row + column * piece_width:base_row + (column + 1) * piece_width], preferred_element_type=jnp.float32) for column in range(slices)])
        hidden = (jax.nn.silu(pre_vals[:, :FF]) * pre_vals[:, FF:]).astype(jnp.bfloat16)
        outputs.append(jnp.dot(hidden, weight_out[:, base_row:base_row + D], preferred_element_type=jnp.float32).astype(jnp.bfloat16))
    stacked = jnp.stack(outputs).reshape(-1, D)
    pair_out = stacked[flat_fwd].reshape(rows_all, TOP, D)
    fwd_result = (values + lax.optimization_barrier(jnp.sum(gate_fwd[:, :, None] * pair_out.astype(jnp.float32), axis=1))).astype(jnp.bfloat16)
    saved_values = saved_in.astype(jnp.float32)
    saved_inv = lax.rsqrt(lax.optimization_barrier(jnp.mean(saved_values * saved_values, axis=-1, keepdims=True)) + epsilon)
    grad_values = grad_in.astype(jnp.float32)
    weighted = (gate_bwd[:, :, None] * grad_values[:, None, :]).astype(jnp.bfloat16).reshape(pair_count, D)
    flat_bwd, inverse_bwd = pair_layout(route_bwd)
    grad_rows = dispatch(weighted, inverse_bwd)
    pre_rows = dispatch(saved_pre.reshape(pair_count, 2 * FF), inverse_bwd)
    grads = []
    for expert in range(EXPERTS):
        grad_now = grad_rows[expert]
        base_row = expert * D
        hidden_grad = pair_total([lax.dot_general(grad_now[:, column * piece_width:(column + 1) * piece_width], weight_out[:, base_row + column * piece_width:base_row + (column + 1) * piece_width], contract, preferred_element_type=jnp.float32) for column in range(slices)])
        pre_vals = pre_rows[expert].astype(jnp.float32)
        gate_pre = pre_vals[:, :FF]
        up_pre = pre_vals[:, FF:]
        sigma = jax.nn.sigmoid(gate_pre)
        slope = sigma * (1.0 + gate_pre * (1.0 - sigma))
        grad_gu = jnp.concatenate([hidden_grad * up_pre * slope, hidden_grad * gate_pre * sigma], axis=1).astype(jnp.bfloat16)
        grads.append(lax.dot_general(grad_gu, weight_in[base_row:base_row + D], contract, preferred_element_type=jnp.float32).astype(jnp.bfloat16))
    stacked_grad = jnp.stack(grads).reshape(-1, D)
    pair_grad = stacked_grad[flat_bwd].reshape(rows_all, TOP, D)
    feature_grad = lax.optimization_barrier(jnp.sum(pair_grad.astype(jnp.float32), axis=1))
    scaled = gain_row * feature_grad
    mean_term = lax.optimization_barrier(jnp.mean(saved_values * scaled, axis=-1, keepdims=True))
    bwd_result = (grad_values + saved_inv * scaled - saved_values * saved_inv ** 3 * mean_term).astype(jnp.bfloat16)
    section_gain = lax.optimization_barrier(jnp.sum(feature_grad * saved_values * saved_inv, axis=0))
    return (fwd_result, bwd_result, section_gain)

def reference(fwd_sent, bwd_sent, bwd_saved, bwd_pre, fwd_route, bwd_route, fwd_gate, bwd_gate, gain, w_in, w_out):
    arrived = jnp.roll(fwd_sent, 1, axis=0)
    returned = jnp.roll(bwd_sent, -1, axis=0)
    fwd_out, bwd_out, section_gain = lax.map(section_step, (arrived, returned, bwd_saved, bwd_pre, fwd_route, bwd_route, fwd_gate, bwd_gate, gain, w_in, w_out))
    gain_grad = section_gain + section_gain[::-1]
    return (fwd_out, bwd_out, gain_grad)
```

```python
import jax
import jax.numpy as jnp
from jax import lax
from jax.experimental import pallas as pl
from jax.experimental.pallas import tpu as pltpu
from jax.sharding import PartitionSpec as P

D = 7168
FF = 1024
CAP = 72
TOK = 128
SLICE = 1792
ROWS = 2 * CAP
TILE = 256
EPS = 1e-06
F32 = jnp.float32
BF16 = jnp.bfloat16
MESH = pl.DeviceIdType.MESH


def kernel(
    meta,
    gain,
    fwd_sent,
    bwd_sent,
    saved,
    pre,
    w_in,
    w_out,
    fwd_out,
    bwd_out,
    local_gain,
    ret_f,
    ret_b,
    w1,
    w2,
    v_f,
    v_b,
    x_f,
    x_b,
    s_f,
    s_b,
    part,
    r1_f,
    r1_b,
    r2_f,
    r2_b,
    h_f,
    h_b,
    xr_f,
    xr_b,
    pre_in,
    pre_out,
    pre_got,
    stage,
    meta_got,
    inv_out,
    inv_got,
    pick_f,
    pick_b,
    pick_pre,
    comb_f,
    comb_b,
    load_sem,
    stage_sem,
    out_sem,
    misc_send,
    misc_recv,
    pre_send,
    pre_recv,
    s1_send,
    s1_recv,
    d_send,
    d_recv,
    r1_send,
    r1_recv,
    r2_send,
    r2_recv,
    ag_send,
    ag_recv,
    ac_send,
    ac_recv,
    ret_send,
    ret_recv,
    x_send,
    x_recv,
):
    p = lax.axis_index("pp")
    ep = lax.axis_index("ep")
    xh = ep // 8
    z = (ep // 2) % 4
    c = ep % 2
    zp = z % 2
    own_row = pl.multiple_of(xh * TOK, TOK)
    other_row = pl.multiple_of((1 - xh) * TOK, TOK)

    def place(dp, dx, dz, dc):
        x2 = (xh + dx) % 2
        z2 = (z + dz) % 4
        c2 = (c + dc) % 2
        return {"pp": (p + dp) % 8, "ep": x2 * 8 + z2 * 2 + c2}

    def remote(src, dst, send, recv, target):
        return pltpu.make_async_remote_copy(
            src_ref=src,
            dst_ref=dst,
            send_sem=send,
            recv_sem=recv,
            device_id=target,
            device_id_type=MESH,
        )

    def columns(dz, dc):
        j = 2 * ((z + dz) % 2) + (c + dc) % 2
        return pl.multiple_of(j * SLICE, TILE)

    pairs = [(0, 1), (1, 0), (1, 1), (0, 0)]

    loads = []
    for q in range(4):
        loads.append(
            pltpu.make_async_copy(
                fwd_sent.at[:, pl.ds(q * SLICE, SLICE)], s_f.at[q, pl.ds(0, TOK)], load_sem.at[q]
            )
        )
    loads.append(pltpu.make_async_copy(pre, pre_in, load_sem.at[4]))
    loads.append(pltpu.make_async_copy(w_in, w1, load_sem.at[5]))
    loads.append(pltpu.make_async_copy(w_out, w2, load_sem.at[6]))
    for load in loads:
        load.start()

    peers = [(1, 0, 0, 0), (1, 1, 0, 0), (7, 0, 0, 0), (7, 1, 0, 0), (0, 1, 0, 0), (0, 1, 2, 0)]
    peers += [(0, 0, dz, dc) for dz in range(4) for dc in range(2) if (dz, dc) != (0, 0)]
    barrier = pltpu.get_barrier_semaphore()
    for peer in peers:
        pl.semaphore_signal(barrier, inc=1, device_id=place(*peer), device_id_type=MESH)
    pl.semaphore_wait(barrier, len(peers))

    meta_copy = remote(meta, meta_got, misc_send.at[0], misc_recv.at[0], place(0, 1, 0, 0))
    meta_copy.start()

    def sent_copies(stream, src, dst, dp):
        made = {}
        for dz, dc in pairs:
            cols = pl.ds(columns(dz, dc), SLICE)
            for dx in range(2):
                made[dz, dc, dx] = remote(
                    src.at[:, cols],
                    dst.at[pl.ds(own_row, TOK), cols],
                    s1_send.at[stream, 2 * dz + dc, dx],
                    s1_recv.at[stream, 2 * dz + dc, dx],
                    place(dp, dx, 0, 0),
                )
        return made

    first_f = sent_copies(0, fwd_sent, v_f, 1)
    first_b = sent_copies(1, bwd_sent, v_b, 7)
    for copy in first_f.values():
        copy.start()

    total = jnp.zeros((TOK, 1), F32)
    for q in range(4):
        loads[q].wait()
        block = s_f[q, pl.ds(0, TOK), :].astype(F32)
        total = total + jnp.sum(block * block, axis=1, keepdims=True)
    inv_out[...] = jnp.broadcast_to(lax.rsqrt(total / D + EPS), (TOK, 128))
    inv_copies = [
        remote(
            inv_out,
            inv_got.at[pl.ds(own_row, TOK)],
            misc_send.at[1 + dx],
            misc_recv.at[1 + dx],
            place(1, dx, 0, 0),
        )
        for dx in range(2)
    ]
    for copy in inv_copies:
        copy.start()
    for copy in first_b.values():
        copy.start()

    meta_copy.wait_recv()
    own_meta = meta[...]
    got_meta = meta_got[...]
    row_id = lax.broadcasted_iota(jnp.int32, (TOK, TOK), 0)
    col_id = lax.broadcasted_iota(jnp.int32, (TOK, TOK), 1)
    before = jnp.where(row_id < col_id, 1.0, 0.0).astype(BF16)

    def slots(block, stream, expert):
        expert = expert.astype(F32)
        hit0 = jnp.where(block[2 * stream : 2 * stream + 1] == expert, 1.0, 0.0)
        hit1 = jnp.where(block[2 * stream + 1 : 2 * stream + 2] == expert, 1.0, 0.0)
        hit = hit0 + hit1
        wide = jnp.broadcast_to(hit, (16, TOK)).astype(BF16)
        slot = jnp.dot(wide, before, preferred_element_type=F32)[0:1]
        gate = (
            block[4 + 2 * stream : 5 + 2 * stream] * hit0
            + block[5 + 2 * stream : 6 + 2 * stream] * hit1
        )
        return hit0, hit1, hit, slot, gate

    for stream, pick, comb in ((0, pick_f, comb_f), (1, pick_b, comb_b)):
        rows_needed = []
        for local in range(2):
            expert = 2 * xh + local
            own = slots(own_meta, stream, expert)
            got = slots(got_meta, stream, expert)
            low = xh == 0
            hit_row = jnp.concatenate(
                [jnp.where(low, own[2], got[2]), jnp.where(low, got[2], own[2])], axis=1
            )
            slot_row = jnp.concatenate(
                [jnp.where(low, own[3], got[3]), jnp.where(low, got[3], own[3]) + CAP], axis=1
            )
            line = lax.broadcasted_iota(jnp.int32, (ROWS, 2 * TOK), 0).astype(F32)
            pick[local] = jnp.where((line == slot_row) & (hit_row > 0.5), 1.0, 0.0).astype(BF16)
            for side in (own, got):
                rows_needed += [side[3], side[4]]
        padding = jnp.zeros((TOK - len(rows_needed), TOK), F32)
        turned = jnp.concatenate(rows_needed + [padding], axis=0).T
        lane = lax.broadcasted_iota(jnp.int32, (TOK, 2 * ROWS), 1).astype(F32)
        for side in range(2):
            home = jnp.where(xh == 0, side, 1 - side).astype(F32)
            mix = jnp.zeros((TOK, 2 * ROWS), F32)
            for local in range(2):
                k = 2 * (2 * local + side)
                slot_col = turned[:, k : k + 1] + (home * CAP + local * ROWS)
                gate_col = turned[:, k + 1 : k + 2]
                mix = mix + jnp.where(lane == slot_col, gate_col, 0.0)
            high = mix.astype(BF16)
            comb[pl.ds(2 * side * TOK, TOK), :] = high
            comb[pl.ds((2 * side + 1) * TOK, TOK), :] = (mix - high.astype(F32)).astype(BF16)

    loads[4].wait()
    pre_copies = {}
    for dx in range(2):
        for i in range(2):
            expert = 2 * ((xh + dx) % 2) + ((z + 2 * i) % 4) // 2
            hit0, hit1, _, slot, _ = slots(own_meta, 1, expert)
            hit_row = jnp.concatenate([hit0, hit1], axis=1)
            slot_row = jnp.concatenate([slot, slot], axis=1)
            line = lax.broadcasted_iota(jnp.int32, (80, 2 * TOK), 0).astype(F32)
            pick_pre[...] = jnp.where((line == slot_row) & (hit_row > 0.5), 1.0, 0.0).astype(BF16)
            target = pre_got.at[i, xh] if (dx, i) == (0, 0) else pre_out.at[2 * dx + i]

            def gather_pre(t, carry, target=target):
                cols = pl.ds(pl.multiple_of(t * 512, 512), 512)
                target[:, cols] = jnp.dot(
                    pick_pre[...], pre_in[:, cols], preferred_element_type=F32
                ).astype(BF16)
                return carry

            lax.fori_loop(0, 4, gather_pre, 0)
            if (dx, i) != (0, 0):
                copy = remote(
                    pre_out.at[2 * dx + i],
                    pre_got.at[i, xh],
                    pre_send.at[i, dx],
                    pre_recv.at[i, dx],
                    place(0, dx, 2 * i, 0),
                )
                copy.start()
                pre_copies[dx, i] = copy

    def dispatch(stream, first, v, pick, s, x):
        made = {}
        for dzp, dc in pairs:
            for dx in range(2):
                first[dzp, dc, dx].wait_recv()
            base = columns(dzp, dc)
            outs = []
            for dz in (dzp, dzp + 2):
                here = x if (dz, dc) == (0, 0) else s
                outs.append((here, dz, ((z + dz) % 4) // 2))

            def gather(t, carry, base=base, outs=outs, dc=dc):
                cols = pl.ds(pl.multiple_of(base + t * TILE, TILE), TILE)
                block = v[:, cols]
                if stream == 0:
                    block = (block.astype(F32) * inv_got[:, 0:1] * gain[:, cols]).astype(BF16)
                where = pl.ds(pl.multiple_of(t * TILE, TILE), TILE)
                for ref, dz, local in outs:
                    ref[dz, pl.ds(dc * ROWS, ROWS), where] = jnp.dot(
                        pick[local], block, preferred_element_type=F32
                    ).astype(BF16)
                return carry

            lax.fori_loop(0, SLICE // TILE, gather, 0)
            for dz in (dzp, dzp + 2):
                if (dz, dc) == (0, 0):
                    continue
                rows = pl.ds(dc * ROWS, ROWS)
                copy = remote(
                    s.at[dz, rows],
                    x.at[dz, rows],
                    d_send.at[stream, dz, dc],
                    d_recv.at[stream, dz, dc],
                    place(0, 0, dz, dc),
                )
                copy.start()
                made[dz, dc] = copy
        return made

    def multiply(lhs, w, out, count, tile, turned):
        def step(t, carry):
            cols = pl.ds(pl.multiple_of(t * tile, tile), tile)
            if turned:
                got = lax.dot_general(
                    lhs[...], w[cols, :], (((1,), (1,)), ((), ())), preferred_element_type=F32
                )
            else:
                got = jnp.dot(lhs[...], w[:, cols], preferred_element_type=F32)
            out[:, cols] = got.astype(BF16)
            return carry

        lax.fori_loop(0, count // tile, step, 0)

    def first_products(stream, sent, x, r1, width):
        made = []
        for dz in range(4):
            for dc in range(2):
                if (dz, dc) != (0, 0):
                    sent[dz, dc].wait_recv()
            out = part.at[dz, :, pl.ds(0, width)]
            if stream == 0:
                multiply(x.at[dz], w1, out, width, 512, False)
            else:
                multiply(x.at[dz], w2, out, width, 512, True)
            copy = remote(
                part.at[dz, pl.ds(ROWS, ROWS), pl.ds(0, width)],
                r1.at[dz],
                r1_send.at[stream, dz],
                r1_recv.at[stream, dz],
                place(0, 0, 0, 1),
            )
            copy.start()
            made.append(copy)
        return made

    partner = {"pp": p, "ep": xh * 8 + (z + 1 - 2 * zp) * 2 + c}

    def chip_sums(stream, crossed, r1, r2, width):
        made = []
        for dz in (1, 3, 0, 2):
            crossed[dz].wait_recv()

            def add(t, carry, dz=dz):
                cols = pl.ds(pl.multiple_of(t * 512, 512), 512)
                rows = pl.ds(0, ROWS)
                part[dz, rows, cols] = (
                    part[dz, rows, cols].astype(F32) + r1[dz, :, cols].astype(F32)
                ).astype(BF16)
                return carry

            lax.fori_loop(0, width // 512, add, 0)
            if dz % 2 == 1:
                index = ((dz + 5 - 2 * zp) % 4) // 2
                copy = remote(
                    part.at[dz, pl.ds(0, ROWS), pl.ds(0, width)],
                    r2.at[index],
                    r2_send.at[stream, dz // 2],
                    r2_recv.at[stream, index],
                    partner,
                )
                copy.start()
                made.append(copy)
        return made

    def landed(stream, r2, width, index):
        return remote(
            part.at[0, pl.ds(0, ROWS), pl.ds(0, width)],
            r2.at[index],
            r2_send.at[stream, 0],
            r2_recv.at[stream, index],
            partner,
        )

    def activate(stream, r2, h, width):
        partner_copies, core_copies = [], {}
        rows = pl.ds(0, ROWS)
        for i in range(2):
            dz = 2 * i
            landed(stream, r2, width, i).wait_recv()
            if stream == 1:
                for dx in range(2):
                    if (dx, i) != (0, 0):
                        pre_copies[dx, i].wait_recv()

            def step(t, carry, i=i, dz=dz):
                lo = pl.ds(pl.multiple_of(t * TILE, TILE), TILE)
                hi = pl.ds(pl.multiple_of(t * TILE + FF, TILE), TILE)
                if stream == 0:
                    g = part[dz, rows, lo].astype(F32) + r2[i, :, lo].astype(F32)
                    u = part[dz, rows, hi].astype(F32) + r2[i, :, hi].astype(F32)
                    h[dz, rows, lo] = (g / (1.0 + jnp.exp(-g)) * u).astype(BF16)
                else:
                    hg = part[dz, rows, lo].astype(F32) + r2[i, :, lo].astype(F32)
                    g = jnp.concatenate(
                        [pre_got[i, k, :, lo].astype(F32)[0:CAP] for k in range(2)], axis=0
                    )
                    u = jnp.concatenate(
                        [pre_got[i, k, :, hi].astype(F32)[0:CAP] for k in range(2)], axis=0
                    )
                    sig = 1.0 / (1.0 + jnp.exp(-g))
                    h[dz, rows, lo] = (hg * u * sig * (1.0 + g * (1.0 - sig))).astype(BF16)
                    h[dz, rows, hi] = (hg * g * sig).astype(BF16)
                return carry

            lax.fori_loop(0, FF // TILE, step, 0)
            there = (dz + 5 - 2 * zp) % 4
            copy = remote(
                h.at[dz, rows],
                h.at[there, rows],
                ag_send.at[stream, i],
                ag_recv.at[stream, there // 2],
                partner,
            )
            copy.start()
            partner_copies.append(copy)
            core_copies[dz] = to_core(stream, h, dz)
            core_copies[dz].start()
        return partner_copies, core_copies

    def to_core(stream, h, dz):
        return remote(
            h.at[dz, pl.ds(0, ROWS)],
            h.at[dz, pl.ds(ROWS, ROWS)],
            ac_send.at[stream, dz],
            ac_recv.at[stream, dz],
            place(0, 0, 0, 1),
        )

    def forward_on(stream, h, core_copies):
        for i in range(2):
            dz = 2 * i + 1
            remote(
                h.at[2 * i, pl.ds(0, ROWS)],
                h.at[dz, pl.ds(0, ROWS)],
                ag_send.at[stream, i],
                ag_recv.at[stream, i],
                partner,
            ).wait_recv()
            core_copies[dz] = to_core(stream, h, dz)
            core_copies[dz].start()

    def second_products(stream, core_copies, h, s, ret):
        made = {}
        local = z // 2
        region = ret.at[
            pl.ds(pl.multiple_of(local * ROWS, ROWS), ROWS), pl.ds(columns(0, 0), SLICE)
        ]
        for dz in (0, 2, 1, 3):
            core_copies[dz].wait_recv()
            if stream == 0:
                multiply(h.at[dz], w2, s.at[dz], SLICE, TILE, False)
            else:
                multiply(h.at[dz], w1, s.at[dz], SLICE, TILE, True)
            for dc in range(2):
                rows = pl.ds(dc * ROWS, ROWS)
                if (dz, dc) == (0, 0):
                    copy = pltpu.make_async_copy(s.at[dz, rows], region, ret_recv.at[stream, 0, 0])
                else:
                    copy = remote(
                        s.at[dz, rows],
                        region,
                        ret_send.at[stream, dz, dc],
                        ret_recv.at[stream, dz, dc],
                        place(0, 0, 4 - dz, dc),
                    )
                copy.start()
                made[dz, dc] = copy
        return made

    def combine(stream, returned, ret, comb, v, x, xr):
        made = {}
        for n, (dzp, dc) in enumerate(pairs):
            for dz in (dzp, dzp + 2):
                if (dz, dc) == (0, 0):
                    returned[dz, dc].wait()
                else:
                    returned[dz, dc].wait_recv()
            base = columns(dzp, dc)
            fetch = pltpu.make_async_copy(
                ret.at[:, pl.ds(base, SLICE)], stage.at[n % 2], stage_sem.at[n % 2]
            )
            fetch.start()
            fetch.wait()
            jr = 2 * dzp + dc

            def step(t, carry, n=n, base=base, jr=jr):
                cols = pl.ds(pl.multiple_of(t * TILE, TILE), TILE)
                mixed = jnp.dot(comb[...], stage[n % 2, :, cols], preferred_element_type=F32)
                own = mixed[0:TOK] + mixed[TOK : 2 * TOK]
                other = mixed[2 * TOK : 3 * TOK] + mixed[3 * TOK :]
                high = own.astype(BF16)
                x[jr, pl.ds(0, TOK), cols] = high
                x[jr, pl.ds(TOK, TOK), cols] = (own - high.astype(F32)).astype(BF16)
                out_cols = pl.ds(pl.multiple_of(base + t * TILE, TILE), TILE)
                v[pl.ds(other_row, TOK), out_cols] = other.astype(BF16)
                return carry

            lax.fori_loop(0, SLICE // TILE, step, 0)
            copy = remote(
                v.at[pl.ds(other_row, TOK), pl.ds(base, SLICE)],
                xr.at[:, pl.ds(base, SLICE)],
                x_send.at[stream, jr],
                x_recv.at[stream, jr],
                place(0, 1, 0, 0),
            )
            copy.start()
            made[dzp, dc] = copy
        return made

    def finish_forward(crossed):
        for dzp, dc in pairs:
            crossed[dzp, dc].wait_recv()
            base = columns(dzp, dc)
            jr = 2 * dzp + dc

            def step(t, carry, base=base, jr=jr):
                cols = pl.ds(pl.multiple_of(t * TILE, TILE), TILE)
                wide = pl.ds(pl.multiple_of(base + t * TILE, TILE), TILE)
                here = pl.ds(own_row, TOK)
                mine = x_f[jr, pl.ds(0, TOK), cols].astype(F32)
                mine = mine + x_f[jr, pl.ds(TOK, TOK), cols].astype(F32)
                v_f[here, wide] = (
                    v_f[here, wide].astype(F32) + (mine + xr_f[:, wide].astype(F32))
                ).astype(BF16)
                return carry

            lax.fori_loop(0, SLICE // TILE, step, 0)
            copy = pltpu.make_async_copy(
                v_f.at[pl.ds(own_row, TOK), pl.ds(base, SLICE)],
                fwd_out.at[:, pl.ds(base, SLICE)],
                out_sem.at[0, jr],
            )
            copy.start()
            outs.append(copy)

    def finish_backward(crossed):
        total = jnp.zeros((TOK, 1), F32)
        for n, (dzp, dc) in enumerate(pairs):
            saved_loads[n].wait()
            block = s_f[2 * dzp + dc, pl.ds(0, TOK), :].astype(F32)
            total = total + jnp.sum(block * block, axis=1, keepdims=True)
        inv = lax.rsqrt(total / D + EPS)
        dots = jnp.zeros((TOK, TILE), F32)
        for dzp, dc in pairs:
            crossed[dzp, dc].wait_recv()
            base = columns(dzp, dc)
            jr = 2 * dzp + dc

            def step(t, carry, base=base, jr=jr):
                cols = pl.ds(pl.multiple_of(t * TILE, TILE), TILE)
                wide = pl.ds(pl.multiple_of(base + t * TILE, TILE), TILE)
                grad = x_b[jr, pl.ds(0, TOK), cols].astype(F32)
                grad = grad + x_b[jr, pl.ds(TOK, TOK), cols].astype(F32)
                grad = grad + xr_b[:, wide].astype(F32)
                high = grad.astype(BF16)
                x_b[jr, pl.ds(0, TOK), cols] = high
                x_b[jr, pl.ds(TOK, TOK), cols] = (grad - high.astype(F32)).astype(BF16)
                w = s_f[jr, pl.ds(0, TOK), cols].astype(F32)
                local_gain[:, wide] = jnp.sum(grad * w * inv, axis=0, keepdims=True)
                return carry + w * gain[:, wide] * grad

            dots = lax.fori_loop(0, SLICE // TILE, step, dots)
        scale = inv * inv * inv * (jnp.sum(dots, axis=1, keepdims=True) / D)
        for dzp, dc in pairs:
            base = columns(dzp, dc)
            jr = 2 * dzp + dc

            def last(t, carry, base=base, jr=jr):
                cols = pl.ds(pl.multiple_of(t * TILE, TILE), TILE)
                wide = pl.ds(pl.multiple_of(base + t * TILE, TILE), TILE)
                here = pl.ds(own_row, TOK)
                grad = x_b[jr, pl.ds(0, TOK), cols].astype(F32)
                grad = grad + x_b[jr, pl.ds(TOK, TOK), cols].astype(F32)
                w = s_f[jr, pl.ds(0, TOK), cols].astype(F32)
                v_b[here, wide] = (
                    v_b[here, wide].astype(F32) + inv * (gain[:, wide] * grad) - w * scale
                ).astype(BF16)
                return carry

            lax.fori_loop(0, SLICE // TILE, last, 0)
            copy = pltpu.make_async_copy(
                v_b.at[pl.ds(own_row, TOK), pl.ds(base, SLICE)],
                bwd_out.at[:, pl.ds(base, SLICE)],
                out_sem.at[1, jr],
            )
            copy.start()
            outs.append(copy)

    def sends_done(copies):
        for copy in copies:
            copy.wait_send()

    outs = []
    for copy in inv_copies:
        copy.wait_recv()
    sent_f = dispatch(0, first_f, v_f, pick_f, s_f, x_f)
    loads[5].wait()
    core_f = first_products(0, sent_f, x_f, r1_f, 2 * FF)
    chip_f = chip_sums(0, core_f, r1_f, r2_f, 2 * FF)
    sent_b = dispatch(1, first_b, v_b, pick_b, s_b, x_b)
    ag_f, ac_f = activate(0, r2_f, h_f, 2 * FF)
    loads[6].wait()
    forward_on(0, h_f, ac_f)
    sends_done(sent_f.values())
    back_f = second_products(0, ac_f, h_f, s_f, ret_f)
    sends_done(core_f + chip_f)
    core_b = first_products(1, sent_b, x_b, r1_b, FF)
    chip_b = chip_sums(1, core_b, r1_b, r2_b, FF)
    over_f = combine(0, back_f, ret_f, comb_f, v_f, x_f, xr_f)
    ag_b, ac_b = activate(1, r2_b, h_b, FF)
    forward_on(1, h_b, ac_b)
    sends_done(sent_b.values())
    back_b = second_products(1, ac_b, h_b, s_b, ret_b)
    sends_done([copy for key, copy in back_f.items() if key != (0, 0)])
    saved_loads = []
    for n, (dzp, dc) in enumerate(pairs):
        copy = pltpu.make_async_copy(
            saved.at[:, pl.ds(columns(dzp, dc), SLICE)],
            s_f.at[2 * dzp + dc, pl.ds(0, TOK)],
            load_sem.at[n],
        )
        copy.start()
        saved_loads.append(copy)
    finish_forward(over_f)
    over_b = combine(1, back_b, ret_b, comb_b, v_b, x_b, xr_b)
    finish_backward(over_b)

    sends_done([meta_copy] + inv_copies + list(pre_copies.values()))
    sends_done(list(first_f.values()) + list(first_b.values()))
    sends_done(core_b + chip_b + ag_f + ag_b)
    sends_done(list(ac_f.values()) + list(ac_b.values()))
    sends_done([copy for key, copy in back_b.items() if key != (0, 0)])
    sends_done(list(over_f.values()) + list(over_b.values()))
    for copy in outs:
        copy.wait()


def on_device(
    fwd_sent,
    bwd_sent,
    bwd_saved,
    bwd_pre,
    fwd_route,
    bwd_route,
    fwd_gate,
    bwd_gate,
    gain,
    w_in,
    w_out,
):
    meta = jnp.concatenate(
        [
            fwd_route[0].T.astype(F32),
            bwd_route[0].T.astype(F32),
            fwd_gate[0].T,
            bwd_gate[0].T,
        ],
        axis=0,
    )
    pre = jnp.transpose(bwd_pre[0], (1, 0, 2)).reshape(2 * TOK, 2 * FF)
    anywhere = pl.BlockSpec(memory_space=pl.ANY)
    vmem = pl.BlockSpec(memory_space=pltpu.VMEM)
    dma = pltpu.SemaphoreType.DMA

    def buf(*shape):
        return pltpu.VMEM(shape, BF16)

    fwd_out, bwd_out, local_gain, _, _ = pl.pallas_call(
        kernel,
        out_shape=(
            jax.ShapeDtypeStruct((TOK, D), BF16),
            jax.ShapeDtypeStruct((TOK, D), BF16),
            jax.ShapeDtypeStruct((1, D), F32),
            jax.ShapeDtypeStruct((2 * ROWS, D), BF16),
            jax.ShapeDtypeStruct((2 * ROWS, D), BF16),
        ),
        in_specs=[vmem, vmem] + [anywhere] * 6,
        out_specs=(anywhere, anywhere, vmem, anywhere, anywhere),
        scratch_shapes=[
            buf(SLICE, 2 * FF),
            buf(FF, SLICE),
            buf(2 * TOK, D),
            buf(2 * TOK, D),
            buf(4, 2 * ROWS, SLICE),
            buf(4, 2 * ROWS, SLICE),
            buf(4, 2 * ROWS, SLICE),
            buf(4, 2 * ROWS, SLICE),
            buf(4, 2 * ROWS, 2 * FF),
            buf(4, ROWS, 2 * FF),
            buf(4, ROWS, FF),
            buf(2, ROWS, 2 * FF),
            buf(2, ROWS, FF),
            buf(4, 2 * ROWS, FF),
            buf(4, 2 * ROWS, 2 * FF),
            buf(TOK, D),
            buf(TOK, D),
            buf(2 * TOK, 2 * FF),
            buf(4, 80, 2 * FF),
            buf(2, 2, 80, 2 * FF),
            buf(2, 2 * ROWS, SLICE),
            pltpu.VMEM((8, TOK), F32),
            pltpu.VMEM((TOK, 128), F32),
            pltpu.VMEM((2 * TOK, 128), F32),
            buf(2, ROWS, 2 * TOK),
            buf(2, ROWS, 2 * TOK),
            buf(80, 2 * TOK),
            buf(4 * TOK, 2 * ROWS),
            buf(4 * TOK, 2 * ROWS),
            dma((8,)),
            dma((2,)),
            dma((2, 4)),
            dma((4,)),
            dma((4,)),
            dma((2, 2)),
            dma((2, 2)),
            dma((2, 4, 2)),
            dma((2, 4, 2)),
            dma((2, 4, 2)),
            dma((2, 4, 2)),
            dma((2, 4)),
            dma((2, 4)),
            dma((2, 2)),
            dma((2, 2)),
            dma((2, 2)),
            dma((2, 2)),
            dma((2, 4)),
            dma((2, 4)),
            dma((2, 4, 2)),
            dma((2, 4, 2)),
            dma((2, 4)),
            dma((2, 4)),
        ],
        compiler_params=pltpu.CompilerParams(
            collective_id=0, has_side_effects=True, vmem_limit_bytes=64 * 2**20 - 2**16
        ),
        cost_estimate=pl.CostEstimate(
            flops=26 * 10**9, bytes_accessed=40 * 10**6, transcendentals=10**6
        ),
        name="experts",
    )(meta, gain, fwd_sent[0], bwd_sent[0], bwd_saved[0], pre, w_in[0], w_out[0])
    section_gain = lax.psum(local_gain, "ep")
    mirrored = lax.ppermute(section_gain, "pp", [(i, 7 - i) for i in range(8)])
    return (fwd_out[None], bwd_out[None], section_gain + mirrored)


def solution(mesh):
    placed = (
        P("pp", "ep", None),
        P("pp", "ep", None),
        P("pp", "ep", None),
        P("pp", "ep", None, None),
        P("pp", "ep", None),
        P("pp", "ep", None),
        P("pp", "ep", None),
        P("pp", "ep", None),
        P("pp", None),
        P("pp", "ep", None),
        P("pp", None, "ep"),
    )
    return jax.shard_map(
        on_device,
        mesh=mesh,
        in_specs=placed,
        out_specs=(P("pp", "ep", None), P("pp", "ep", None), P("pp", None)),
        check_vma=False,
    )
```

```python
import jax
import jax.numpy as jnp
from jax import lax
from jax.experimental import pallas as pl
from jax.experimental.pallas import tpu as pltpu
from jax.sharding import PartitionSpec as P

D = 7168
FF = 1024
CAP = 72
TOK = 128
SLICE = 1792
PART = 896
ROWS = 2 * CAP
TILE = 256
EPS = 1e-06
F32 = jnp.float32
BF16 = jnp.bfloat16
MESH = pl.DeviceIdType.MESH


def kernel(
    meta,
    gain,
    fwd_sent,
    bwd_sent,
    saved,
    pre,
    w_in,
    w_out,
    fwd_out,
    bwd_out,
    gain_grad,
    ret_f,
    ret_b,
    local_gain,
    w1,
    w2,
    v_f,
    v_b,
    x_f,
    x_b,
    s_f,
    s_b,
    part,
    r1_f,
    r1_b,
    r2_f,
    r2_b,
    h_f,
    h_b,
    xr_f,
    xr_b,
    pre_in,
    pre_out,
    pre_got,
    stage,
    meta_got,
    inv_out,
    inv_got,
    pick_f,
    pick_b,
    pick_pre,
    comb_f,
    comb_b,
    load_sem,
    stage_sem,
    out_sem,
    misc_send,
    misc_recv,
    pre_send,
    pre_recv,
    relay,
    near_send,
    far_send,
    relay_send,
    relay_recv,
    s1_recv,
    gain_got,
    gain_sum,
    gain_send,
    gain_recv,
    d_send,
    d_recv,
    r1_send,
    r1_recv,
    r2_send,
    r2_recv,
    ag_send,
    ag_recv,
    ac_send,
    ac_recv,
    ret_send,
    ret_recv,
    x_send,
    x_recv,
):
    p = lax.axis_index("pp")
    ep = lax.axis_index("ep")
    xh = ep // 8
    z = (ep // 2) % 4
    c = ep % 2
    zp = z % 2
    own_row = pl.multiple_of(xh * TOK, TOK)
    other_row = pl.multiple_of((1 - xh) * TOK, TOK)

    def place(section, dx, dz, dc):
        x2 = (xh + dx) % 2
        z2 = (z + dz) % 4
        c2 = (c + dc) % 2
        return {"pp": section, "ep": x2 * 8 + z2 * 2 + c2}

    def remote(src, dst, send, recv, target):
        return pltpu.make_async_remote_copy(
            src_ref=src,
            dst_ref=dst,
            send_sem=send,
            recv_sem=recv,
            device_id=target,
            device_id_type=MESH,
        )

    def columns(dz, dc):
        j = 2 * ((z + dz) % 2) + (c + dc) % 2
        return pl.multiple_of(j * SLICE, TILE)

    pairs = [(1, 0), (1, 1), (0, 1), (0, 0)]
    even = p % 2 == 0
    near = p + 1 - 2 * (p % 2)
    ahead = (p + 6 + 4 * (p % 2)) % 8

    loads = []
    for q in range(4):
        loads.append(
            pltpu.make_async_copy(
                fwd_sent.at[:, pl.ds(q * SLICE, SLICE)], s_f.at[q, pl.ds(0, TOK)], load_sem.at[q]
            )
        )
    loads.append(pltpu.make_async_copy(pre, pre_in, load_sem.at[4]))
    loads.append(pltpu.make_async_copy(w_in, w1, load_sem.at[5]))
    loads.append(pltpu.make_async_copy(w_out, w2, load_sem.at[6]))
    for load in loads:
        load.start()

    peers = [(near, 0, 0, 0), (near, 1, 0, 0), (7 - p, 0, 0, 0), (7 - p, 1, 0, 0)]
    peers += [((p + 2) % 8, 0, 0, 0), ((p + 6) % 8, 0, 0, 0), (p, 1, 0, 0), (p, 1, 2, 0)]
    far = (p + 7 + 2 * (p % 2)) % 8
    peers += [(far, 0, 0, 0), (far, 1, 0, 0)]
    peers += [(p, 0, dz, dc) for dz in range(4) for dc in range(2) if (dz, dc) != (0, 0)]
    barrier = pltpu.get_barrier_semaphore()
    for peer in peers:
        pl.semaphore_signal(barrier, inc=1, device_id=place(*peer), device_id_type=MESH)
    pl.semaphore_wait(barrier, len(peers))

    meta_copy = remote(meta, meta_got, misc_send.at[0], misc_recv.at[0], place(p, 1, 0, 0))
    meta_copy.start()

    def block_copies(src, dst, send, recv, dz, dc, stream):
        cols = pl.ds(columns(dz, dc), SLICE)
        jr = 2 * dz + dc
        return [
            remote(
                src.at[:, cols],
                dst.at[pl.ds(own_row, TOK), cols],
                send.at[jr, dx],
                recv.at[stream, jr, dx],
                place(near, dx, 0, 0),
            )
            for dx in range(2)
        ]

    def relay_copy(src, dz, dc):
        cols = pl.ds(columns(dz, dc), SLICE)
        jr = 2 * dz + dc
        return remote(
            src.at[:, cols],
            relay.at[:, cols],
            relay_send.at[jr],
            relay_recv.at[jr],
            place(ahead, 0, 0, 0),
        )

    def start_forward(pair):
        @pl.when(even)
        def _():
            for copy in block_copies(fwd_sent, v_f, near_send, s1_recv, *pair, 0):
                copy.start()

        @pl.when(jnp.logical_not(even))
        def _():
            relay_copy(fwd_sent, *pair).start()

    def relay_forward(pair):
        @pl.when(jnp.logical_not(even))
        def _():
            relay_copy(fwd_sent, *pair).wait_recv()
            for copy in block_copies(relay, v_f, far_send, s1_recv, *pair, 0):
                copy.start()

    def start_backward(pair):
        @pl.when(even)
        def _():
            relay_copy(bwd_sent, *pair).start()

    def relay_backward(pair):
        @pl.when(even)
        def _():
            relay_copy(bwd_sent, *pair).wait_recv()
            for copy in block_copies(relay, v_b, far_send, s1_recv, *pair, 1):
                copy.start()

        @pl.when(jnp.logical_not(even))
        def _():
            for copy in block_copies(bwd_sent, v_b, near_send, s1_recv, *pair, 1):
                copy.start()

    def arrived(stream, v, pair):
        for copy in block_copies(fwd_sent, v, near_send, s1_recv, *pair, stream):
            copy.wait_recv()

    for pair in pairs[:2]:
        start_forward(pair)
    for pair in pairs:
        start_backward(pair)

    total = jnp.zeros((TOK, 1), F32)
    for q in range(4):
        loads[q].wait()
        block = s_f[q, pl.ds(0, TOK), :].astype(F32)
        total = total + jnp.sum(block * block, axis=1, keepdims=True)
    inv_out[...] = jnp.broadcast_to(lax.rsqrt(total / D + EPS), (TOK, 128))
    inv_copies = [
        remote(
            inv_out,
            inv_got.at[pl.ds(own_row, TOK)],
            misc_send.at[1 + dx],
            misc_recv.at[1 + dx],
            place((p + 1) % 8, dx, 0, 0),
        )
        for dx in range(2)
    ]
    for copy in inv_copies:
        copy.start()

    meta_copy.wait_recv()
    own_meta = meta[...]
    got_meta = meta_got[...]
    row_id = lax.broadcasted_iota(jnp.int32, (TOK, TOK), 0)
    col_id = lax.broadcasted_iota(jnp.int32, (TOK, TOK), 1)
    before = jnp.where(row_id < col_id, 1.0, 0.0).astype(BF16)

    def slots(block, stream, expert):
        expert = expert.astype(F32)
        hit0 = jnp.where(block[2 * stream : 2 * stream + 1] == expert, 1.0, 0.0)
        hit1 = jnp.where(block[2 * stream + 1 : 2 * stream + 2] == expert, 1.0, 0.0)
        hit = hit0 + hit1
        wide = jnp.broadcast_to(hit, (16, TOK)).astype(BF16)
        slot = jnp.dot(wide, before, preferred_element_type=F32)[0:1]
        gate = (
            block[4 + 2 * stream : 5 + 2 * stream] * hit0
            + block[5 + 2 * stream : 6 + 2 * stream] * hit1
        )
        return hit0, hit1, hit, slot, gate

    for stream, pick, comb in ((0, pick_f, comb_f), (1, pick_b, comb_b)):
        rows_needed = []
        for local in range(2):
            expert = 2 * xh + local
            own = slots(own_meta, stream, expert)
            got = slots(got_meta, stream, expert)
            low = xh == 0
            hit_row = jnp.concatenate(
                [jnp.where(low, own[2], got[2]), jnp.where(low, got[2], own[2])], axis=1
            )
            slot_row = jnp.concatenate(
                [jnp.where(low, own[3], got[3]), jnp.where(low, got[3], own[3]) + CAP], axis=1
            )
            line = lax.broadcasted_iota(jnp.int32, (ROWS, 2 * TOK), 0).astype(F32)
            pick[local] = jnp.where((line == slot_row) & (hit_row > 0.5), 1.0, 0.0).astype(BF16)
            for side in (own, got):
                rows_needed += [side[3], side[4]]
        padding = jnp.zeros((TOK - len(rows_needed), TOK), F32)
        turned = jnp.concatenate(rows_needed + [padding], axis=0).T
        lane = lax.broadcasted_iota(jnp.int32, (TOK, 2 * ROWS), 1).astype(F32)
        for side in range(2):
            home = jnp.where(xh == 0, side, 1 - side).astype(F32)
            mix = jnp.zeros((TOK, 2 * ROWS), F32)
            for local in range(2):
                k = 2 * (2 * local + side)
                slot_col = turned[:, k : k + 1] + (home * CAP + local * ROWS)
                gate_col = turned[:, k + 1 : k + 2]
                mix = mix + jnp.where(lane == slot_col, gate_col, 0.0)
            high = mix.astype(BF16)
            comb[pl.ds(2 * side * TOK, TOK), :] = high
            comb[pl.ds((2 * side + 1) * TOK, TOK), :] = (mix - high.astype(F32)).astype(BF16)

    loads[4].wait()
    pre_copies = {}
    for dx in range(2):
        for i in range(2):
            expert = 2 * ((xh + dx) % 2) + ((z + 2 * i) % 4) // 2
            hit0, hit1, _, slot, _ = slots(own_meta, 1, expert)
            hit_row = jnp.concatenate([hit0, hit1], axis=1)
            slot_row = jnp.concatenate([slot, slot], axis=1)
            line = lax.broadcasted_iota(jnp.int32, (80, 2 * TOK), 0).astype(F32)
            pick_pre[...] = jnp.where((line == slot_row) & (hit_row > 0.5), 1.0, 0.0).astype(BF16)
            target = pre_got.at[i, xh] if (dx, i) == (0, 0) else pre_out.at[2 * dx + i]

            def gather_pre(t, carry, target=target):
                cols = pl.ds(pl.multiple_of(t * 512, 512), 512)
                target[:, cols] = jnp.dot(
                    pick_pre[...], pre_in[:, cols], preferred_element_type=F32
                ).astype(BF16)
                return carry

            lax.fori_loop(0, 4, gather_pre, 0)
            if (dx, i) != (0, 0):
                copy = remote(
                    pre_out.at[2 * dx + i],
                    pre_got.at[i, xh],
                    pre_send.at[i, dx],
                    pre_recv.at[i, dx],
                    place(p, dx, 2 * i, 0),
                )
                copy.start()
                pre_copies[dx, i] = copy

    rows0, rows1 = pl.ds(0, ROWS), pl.ds(ROWS, ROWS)
    partner = {"pp": p, "ep": xh * 8 + (z + 1 - 2 * zp) * 2 + c}
    fwd = dict(
        v=v_f, x=x_f, s=s_f, h=h_f, r1=r1_f, r2=r2_f, ret=ret_f, xr=xr_f, pick=pick_f, comb=comb_f
    )
    bwd = dict(
        v=v_b, x=x_b, s=s_b, h=h_b, r1=r1_b, r2=r2_b, ret=ret_b, xr=xr_b, pick=pick_b, comb=comb_b
    )
    fwd.update(number=0, width=2 * FF)
    bwd.update(number=1, width=FF)
    for stream in (fwd, bwd):
        for name in ("sent", "core", "chip", "ag", "ac", "back", "over"):
            stream[name] = {}

    def dispatch(stream, dzp, dc):
        number, v, s, x = stream["number"], stream["v"], stream["s"], stream["x"]
        base = columns(dzp, dc)
        targets = []
        for dz in (dzp, dzp + 2):
            here = x if (dz, dc) == (0, 0) else s
            targets.append((here, dz, ((z + dz) % 4) // 2))

        def gather(t, carry):
            cols = pl.ds(pl.multiple_of(base + t * TILE, TILE), TILE)
            block = v[:, cols]
            if number == 0:
                block = (block.astype(F32) * inv_got[:, 0:1] * gain[:, cols]).astype(BF16)
            where = pl.ds(pl.multiple_of(t * TILE, TILE), TILE)
            for ref, dz, local in targets:
                ref[dz, pl.ds(dc * ROWS, ROWS), where] = jnp.dot(
                    stream["pick"][local], block, preferred_element_type=F32
                ).astype(BF16)
            return carry

        lax.fori_loop(0, SLICE // TILE, gather, 0)
        for dz in (dzp + 2, dzp):
            if (dz, dc) == (0, 0):
                continue
            rows = pl.ds(dc * ROWS, ROWS)
            copy = remote(
                s.at[dz, rows],
                x.at[dz, rows],
                d_send.at[number, dz, dc],
                d_recv.at[number, dz, dc],
                place(p, 0, dz, dc),
            )
            copy.start()
            stream["sent"][dz, dc] = copy

    def multiply(lhs, w, out, count, tile, turned):
        def step(t, carry):
            cols = pl.ds(pl.multiple_of(t * tile, tile), tile)
            if turned:
                got = lax.dot_general(
                    lhs[...], w[cols, :], (((1,), (1,)), ((), ())), preferred_element_type=F32
                )
            else:
                got = jnp.dot(lhs[...], w[:, cols], preferred_element_type=F32)
            out[:, cols] = got.astype(BF16)
            return carry

        lax.fori_loop(0, count // tile, step, 0)

    def first_product(stream, dz):
        number, x, width = stream["number"], stream["x"], stream["width"]
        for dc in range(2):
            if (dz, dc) != (0, 0):
                stream["sent"][dz, dc].wait_recv()
        out = part.at[dz, :, pl.ds(0, width)]
        if number == 0:
            multiply(x.at[dz], w1, out, width, 512, False)
        else:
            multiply(x.at[dz], w2, out, width, 512, True)
        copy = remote(
            part.at[dz, rows1, pl.ds(0, width)],
            stream["r1"].at[dz],
            r1_send.at[number, dz],
            r1_recv.at[number, dz],
            place(p, 0, 0, 1),
        )
        copy.start()
        stream["core"][dz] = copy

    def chip_sum(stream, dz):
        number, r1, width = stream["number"], stream["r1"], stream["width"]
        stream["core"][dz].wait_recv()

        def add(t, carry):
            cols = pl.ds(pl.multiple_of(t * 512, 512), 512)
            part[dz, rows0, cols] = (
                part[dz, rows0, cols].astype(F32) + r1[dz, :, cols].astype(F32)
            ).astype(BF16)
            return carry

        lax.fori_loop(0, width // 512, add, 0)
        if dz % 2 == 1:
            index = ((dz + 5 - 2 * zp) % 4) // 2
            copy = remote(
                part.at[dz, rows0, pl.ds(0, width)],
                stream["r2"].at[index],
                r2_send.at[number, dz // 2],
                r2_recv.at[number, index],
                partner,
            )
            copy.start()
            stream["chip"][dz] = copy

    def to_core(stream, dz):
        number, h = stream["number"], stream["h"]
        copy = remote(
            h.at[dz, rows0],
            h.at[dz, rows1],
            ac_send.at[number, dz],
            ac_recv.at[number, dz],
            place(p, 0, 0, 1),
        )
        copy.start()
        stream["ac"][dz] = copy

    def activate(stream, dz):
        number, h, r2, width = stream["number"], stream["h"], stream["r2"], stream["width"]
        i = dz // 2
        remote(
            part.at[0, rows0, pl.ds(0, width)],
            r2.at[i],
            r2_send.at[number, 0],
            r2_recv.at[number, i],
            partner,
        ).wait_recv()
        if number == 1:
            for dx in range(2):
                if (dx, i) != (0, 0):
                    pre_copies[dx, i].wait_recv()

        def step(t, carry):
            lo = pl.ds(pl.multiple_of(t * TILE, TILE), TILE)
            hi = pl.ds(pl.multiple_of(t * TILE + FF, TILE), TILE)
            if number == 0:
                g = part[dz, rows0, lo].astype(F32) + r2[i, :, lo].astype(F32)
                u = part[dz, rows0, hi].astype(F32) + r2[i, :, hi].astype(F32)
                h[dz, rows0, lo] = (g / (1.0 + jnp.exp(-g)) * u).astype(BF16)
            else:
                hg = part[dz, rows0, lo].astype(F32) + r2[i, :, lo].astype(F32)
                g = jnp.concatenate(
                    [pre_got[i, k, :, lo].astype(F32)[0:CAP] for k in range(2)], axis=0
                )
                u = jnp.concatenate(
                    [pre_got[i, k, :, hi].astype(F32)[0:CAP] for k in range(2)], axis=0
                )
                sig = 1.0 / (1.0 + jnp.exp(-g))
                h[dz, rows0, lo] = (hg * u * sig * (1.0 + g * (1.0 - sig))).astype(BF16)
                h[dz, rows0, hi] = (hg * g * sig).astype(BF16)
            return carry

        lax.fori_loop(0, FF // TILE, step, 0)
        there = (dz + 5 - 2 * zp) % 4
        copy = remote(
            h.at[dz, rows0],
            h.at[there, rows0],
            ag_send.at[number, i],
            ag_recv.at[number, there // 2],
            partner,
        )
        copy.start()
        stream["ag"][dz] = copy
        to_core(stream, dz)

    def forward_on(stream, dz):
        number, h = stream["number"], stream["h"]
        i = dz // 2
        remote(
            h.at[dz - 1, rows0],
            h.at[dz, rows0],
            ag_send.at[number, i],
            ag_recv.at[number, i],
            partner,
        ).wait_recv()
        to_core(stream, dz)

    def second_product(stream, dz):
        number, h, s, ret = stream["number"], stream["h"], stream["s"], stream["ret"]
        region = ret.at[
            pl.ds(pl.multiple_of(z // 2 * ROWS, ROWS), ROWS), pl.ds(columns(0, 0), SLICE)
        ]
        stream["ac"][dz].wait_recv()
        for dc in range(2):
            if (dz, dc) != (0, 0):
                stream["sent"][dz, dc].wait_send()
        if number == 0:
            multiply(h.at[dz], w2, s.at[dz], SLICE, TILE, False)
        else:
            multiply(h.at[dz], w1, s.at[dz], SLICE, TILE, True)
        for dc in range(2):
            rows = pl.ds(dc * ROWS, ROWS)
            if (dz, dc) == (0, 0):
                copy = pltpu.make_async_copy(s.at[dz, rows], region, ret_recv.at[number, 0, 0])
            else:
                copy = remote(
                    s.at[dz, rows],
                    region,
                    ret_send.at[number, dz, dc],
                    ret_recv.at[number, dz, dc],
                    place(p, 0, 4 - dz, dc),
                )
            copy.start()
            stream["back"][dz, dc] = copy

    def combine(stream, dzp):
        number, v, x, ret = stream["number"], stream["v"], stream["x"], stream["ret"]
        fetches = []
        for dc in (1, 0):
            for dz in (dzp, dzp + 2):
                if (dz, dc) == (0, 0):
                    stream["back"][dz, dc].wait()
                else:
                    stream["back"][dz, dc].wait_recv()
            fetch = pltpu.make_async_copy(
                ret.at[:, pl.ds(columns(dzp, dc), SLICE)], stage.at[dc], stage_sem.at[dc]
            )
            fetch.start()
            fetches.append(fetch)
        for dc in (1, 0):
            fetches[1 - dc].wait()
            base = columns(dzp, dc)
            jr = 2 * dzp + dc

            def step(t, carry, dc=dc, base=base, jr=jr):
                cols = pl.ds(pl.multiple_of(t * TILE, TILE), TILE)
                mixed = jnp.dot(
                    stream["comb"][...], stage[dc, :, cols], preferred_element_type=F32
                )
                own = mixed[0:TOK] + mixed[TOK : 2 * TOK]
                other = mixed[2 * TOK : 3 * TOK] + mixed[3 * TOK :]
                high = own.astype(BF16)
                x[jr, pl.ds(0, TOK), cols] = high
                x[jr, pl.ds(TOK, TOK), cols] = (own - high.astype(F32)).astype(BF16)
                out_cols = pl.ds(pl.multiple_of(base + t * TILE, TILE), TILE)
                v[pl.ds(other_row, TOK), out_cols] = other.astype(BF16)
                return carry

            lax.fori_loop(0, SLICE // TILE, step, 0)
            copy = remote(
                v.at[pl.ds(other_row, TOK), pl.ds(base, SLICE)],
                stream["xr"].at[:, pl.ds(base, SLICE)],
                x_send.at[number, jr],
                x_recv.at[number, jr],
                place(p, 1, 0, 0),
            )
            copy.start()
            stream["over"][dzp, dc] = copy

    late = [(0, 1), (0, 0), (1, 1), (1, 0)]

    def finish_forward(crossed):
        for dzp, dc in late:
            crossed[dzp, dc].wait_recv()
            base = columns(dzp, dc)
            jr = 2 * dzp + dc

            def step(t, carry, base=base, jr=jr):
                cols = pl.ds(pl.multiple_of(t * TILE, TILE), TILE)
                wide = pl.ds(pl.multiple_of(base + t * TILE, TILE), TILE)
                here = pl.ds(own_row, TOK)
                mine = x_f[jr, pl.ds(0, TOK), cols].astype(F32)
                mine = mine + x_f[jr, pl.ds(TOK, TOK), cols].astype(F32)
                v_f[here, wide] = (
                    v_f[here, wide].astype(F32) + (mine + xr_f[:, wide].astype(F32))
                ).astype(BF16)
                return carry

            lax.fori_loop(0, SLICE // TILE, step, 0)
            copy = pltpu.make_async_copy(
                v_f.at[pl.ds(own_row, TOK), pl.ds(base, SLICE)],
                fwd_out.at[:, pl.ds(base, SLICE)],
                out_sem.at[0, jr],
            )
            copy.start()
            outs.append(copy)

    def finish_backward(crossed):
        total = jnp.zeros((TOK, 1), F32)
        for n, (dzp, dc) in enumerate(late):
            saved_loads[n].wait()
            block = s_f[2 * dzp + dc, pl.ds(0, TOK), :].astype(F32)
            total = total + jnp.sum(block * block, axis=1, keepdims=True)
        inv = lax.rsqrt(total / D + EPS)
        dots = jnp.zeros((TOK, TILE), F32)
        for dzp, dc in late:
            crossed[dzp, dc].wait_recv()
            base = columns(dzp, dc)
            jr = 2 * dzp + dc

            def step(t, carry, base=base, jr=jr):
                cols = pl.ds(pl.multiple_of(t * TILE, TILE), TILE)
                wide = pl.ds(pl.multiple_of(base + t * TILE, TILE), TILE)
                grad = x_b[jr, pl.ds(0, TOK), cols].astype(F32)
                grad = grad + x_b[jr, pl.ds(TOK, TOK), cols].astype(F32)
                grad = grad + xr_b[:, wide].astype(F32)
                high = grad.astype(BF16)
                x_b[jr, pl.ds(0, TOK), cols] = high
                x_b[jr, pl.ds(TOK, TOK), cols] = (grad - high.astype(F32)).astype(BF16)
                w = s_f[jr, pl.ds(0, TOK), cols].astype(F32)
                local_gain[:, wide] = jnp.sum(grad * w * inv, axis=0, keepdims=True)
                return carry + w * gain[:, wide] * grad

            dots = lax.fori_loop(0, SLICE // TILE, step, dots)
        scale = inv * inv * inv * (jnp.sum(dots, axis=1, keepdims=True) / D)
        waiting = gain_cores()
        for n, (dzp, dc) in enumerate(late):
            if n == 1:
                waiting = gain_sides(waiting)
            if n == 2:
                waiting = gain_spread(waiting)
            base = columns(dzp, dc)
            jr = 2 * dzp + dc

            def last(t, carry, base=base, jr=jr):
                cols = pl.ds(pl.multiple_of(t * TILE, TILE), TILE)
                wide = pl.ds(pl.multiple_of(base + t * TILE, TILE), TILE)
                here = pl.ds(own_row, TOK)
                grad = x_b[jr, pl.ds(0, TOK), cols].astype(F32)
                grad = grad + x_b[jr, pl.ds(TOK, TOK), cols].astype(F32)
                w = s_f[jr, pl.ds(0, TOK), cols].astype(F32)
                v_b[here, wide] = (
                    v_b[here, wide].astype(F32) + inv * (gain[:, wide] * grad) - w * scale
                ).astype(BF16)
                return carry

            lax.fori_loop(0, SLICE // TILE, last, 0)
            copy = pltpu.make_async_copy(
                v_b.at[pl.ds(own_row, TOK), pl.ds(base, SLICE)],
                bwd_out.at[:, pl.ds(base, SLICE)],
                out_sem.at[1, jr],
            )
            copy.start()
            outs.append(copy)
        for copy in waiting:
            copy.wait_recv()

    half = pl.multiple_of(c * 4 * PART, 128)
    half_other = pl.multiple_of((1 - c) * 4 * PART, 128)
    gain_copies = []

    def send_gain(src, dst, index, target):
        copy = remote(src, dst, gain_send.at[index], gain_recv.at[index], target)
        copy.start()
        gain_copies.append(copy)
        return copy

    def piece(dz):
        return pl.ds(pl.multiple_of(half + (z + dz) % 4 * PART, 128), PART)

    def gain_cores():
        size = pl.ds(half_other, 4 * PART)
        copy = send_gain(local_gain.at[:, size], gain_got.at[:, size], 0, place(p, 0, 0, 1))
        copy.wait_recv()
        size = pl.ds(half, 4 * PART)
        local_gain[:, size] = local_gain[:, size] + gain_got[:, size]
        return [
            send_gain(
                local_gain.at[:, piece(dz)], gain_sum.at[pl.ds(dz, 1)], dz, place(p, 0, dz, 0)
            )
            for dz in range(1, 4)
        ]

    def gain_sides(copies):
        for copy in copies:
            copy.wait_recv()
        mine = local_gain[:, piece(0)]
        for dz in range(1, 4):
            mine = mine + gain_sum[pl.ds(dz, 1)]
        gain_sum[0:1] = mine
        targets = [place(p, 1, 0, 0), place(7 - p, 0, 0, 0), place(7 - p, 1, 0, 0)]
        return [
            send_gain(gain_sum.at[pl.ds(0, 1)], gain_sum.at[pl.ds(4 + i, 1)], 4 + i, target)
            for i, target in enumerate(targets)
        ]

    def gain_spread(copies):
        for copy in copies:
            copy.wait_recv()
        here = gain_sum[0:1] + gain_sum[4:5]
        gain_grad[:, piece(0)] = here + (gain_sum[5:6] + gain_sum[6:7])
        return [
            send_gain(
                gain_grad.at[:, piece(0)],
                gain_grad.at[:, piece(0)],
                8 + 2 * dz + dc,
                place(p, 0, dz, dc),
            )
            for dz in range(4)
            for dc in range(2)
            if (dz, dc) != (0, 0)
        ]

    def sends_done(copies):
        for copy in copies:
            copy.wait_send()

    outs = []
    for copy in inv_copies:
        copy.wait_recv()

    def dispatch_forward(n):
        relay_forward(pairs[n])
        arrived(0, v_f, pairs[n])
        if n + 2 < 4:
            start_forward(pairs[n + 2])
        else:
            relay_backward(pairs[n - 2])
        dispatch(fwd, *pairs[n])

    def dispatch_backward(n):
        arrived(1, v_b, pairs[n])
        dispatch(bwd, *pairs[n])

    def first_product_again(dz):
        fwd["core"][dz].wait_send()
        if dz % 2 == 1:
            fwd["chip"][dz].wait_send()
        first_product(bwd, dz)

    dispatch_forward(0)
    dispatch_forward(1)
    dispatch_forward(2)
    loads[5].wait()
    first_product(fwd, 1)
    first_product(fwd, 3)
    dispatch_forward(3)
    chip_sum(fwd, 1)
    chip_sum(fwd, 3)
    relay_backward(pairs[2])
    relay_backward(pairs[3])
    first_product(fwd, 0)
    first_product(fwd, 2)
    chip_sum(fwd, 0)
    chip_sum(fwd, 2)
    loads[6].wait()
    dispatch_backward(0)
    dispatch_backward(1)
    activate(fwd, 0)
    activate(fwd, 2)
    dispatch_backward(2)
    second_product(fwd, 0)
    second_product(fwd, 2)
    first_product_again(1)
    first_product_again(3)
    forward_on(fwd, 1)
    forward_on(fwd, 3)
    dispatch_backward(3)
    second_product(fwd, 1)
    second_product(fwd, 3)
    chip_sum(bwd, 1)
    chip_sum(bwd, 3)
    first_product_again(0)
    first_product_again(2)
    chip_sum(bwd, 0)
    chip_sum(bwd, 2)
    combine(fwd, 0)
    activate(bwd, 0)
    activate(bwd, 2)
    combine(fwd, 1)
    second_product(bwd, 0)
    second_product(bwd, 2)
    forward_on(bwd, 1)
    forward_on(bwd, 3)
    second_product(bwd, 1)
    second_product(bwd, 3)
    sends_done([copy for key, copy in fwd["back"].items() if key != (0, 0)])
    saved_loads = []
    for n, (dzp, dc) in enumerate(late):
        copy = pltpu.make_async_copy(
            saved.at[:, pl.ds(columns(dzp, dc), SLICE)],
            s_f.at[2 * dzp + dc, pl.ds(0, TOK)],
            load_sem.at[n],
        )
        copy.start()
        saved_loads.append(copy)
    combine(bwd, 0)
    combine(bwd, 1)
    finish_forward(fwd["over"])
    finish_backward(bwd["over"])

    sends_done([meta_copy] + inv_copies + list(pre_copies.values()) + gain_copies)
    for pair in pairs:
        relay_copy(fwd_sent, *pair).wait_send()
        for copy in block_copies(fwd_sent, v_f, near_send, s1_recv, *pair, 0):
            copy.wait_send()
        for copy in block_copies(relay, v_f, far_send, s1_recv, *pair, 0):
            copy.wait_send()
    for stream in (fwd, bwd):
        for name in ("ag", "ac", "over"):
            sends_done(stream[name].values())
    for name in ("core", "chip"):
        sends_done(bwd[name].values())
    sends_done([copy for key, copy in bwd["back"].items() if key != (0, 0)])
    for copy in outs:
        copy.wait()


def on_device(
    fwd_sent,
    bwd_sent,
    bwd_saved,
    bwd_pre,
    fwd_route,
    bwd_route,
    fwd_gate,
    bwd_gate,
    gain,
    w_in,
    w_out,
):
    meta = jnp.concatenate(
        [
            fwd_route[0].T.astype(F32),
            bwd_route[0].T.astype(F32),
            fwd_gate[0].T,
            bwd_gate[0].T,
        ],
        axis=0,
    )
    pre = jnp.transpose(bwd_pre[0], (1, 0, 2)).reshape(2 * TOK, 2 * FF)
    anywhere = pl.BlockSpec(memory_space=pl.ANY)
    vmem = pl.BlockSpec(memory_space=pltpu.VMEM)
    dma = pltpu.SemaphoreType.DMA

    def buf(*shape):
        return pltpu.VMEM(shape, BF16)

    fwd_out, bwd_out, gain_grad, _, _ = pl.pallas_call(
        kernel,
        out_shape=(
            jax.ShapeDtypeStruct((TOK, D), BF16),
            jax.ShapeDtypeStruct((TOK, D), BF16),
            jax.ShapeDtypeStruct((1, D), F32),
            jax.ShapeDtypeStruct((2 * ROWS, D), BF16),
            jax.ShapeDtypeStruct((2 * ROWS, D), BF16),
        ),
        in_specs=[vmem, vmem] + [anywhere] * 6,
        out_specs=(anywhere, anywhere, vmem, anywhere, anywhere),
        scratch_shapes=[
            pltpu.VMEM((1, D), F32),
            buf(SLICE, 2 * FF),
            buf(FF, SLICE),
            buf(2 * TOK, D),
            buf(2 * TOK, D),
            buf(4, 2 * ROWS, SLICE),
            buf(4, 2 * ROWS, SLICE),
            buf(4, 2 * ROWS, SLICE),
            buf(4, 2 * ROWS, SLICE),
            buf(4, 2 * ROWS, 2 * FF),
            buf(4, ROWS, 2 * FF),
            buf(4, ROWS, FF),
            buf(2, ROWS, 2 * FF),
            buf(2, ROWS, FF),
            buf(4, 2 * ROWS, FF),
            buf(4, 2 * ROWS, 2 * FF),
            buf(TOK, D),
            buf(TOK, D),
            buf(2 * TOK, 2 * FF),
            buf(4, 80, 2 * FF),
            buf(2, 2, 80, 2 * FF),
            buf(2, 2 * ROWS, SLICE),
            pltpu.VMEM((8, TOK), F32),
            pltpu.VMEM((TOK, 128), F32),
            pltpu.VMEM((2 * TOK, 128), F32),
            buf(2, ROWS, 2 * TOK),
            buf(2, ROWS, 2 * TOK),
            buf(80, 2 * TOK),
            buf(4 * TOK, 2 * ROWS),
            buf(4 * TOK, 2 * ROWS),
            dma((8,)),
            dma((2,)),
            dma((2, 4)),
            dma((4,)),
            dma((4,)),
            dma((2, 2)),
            dma((2, 2)),
            buf(TOK, D),
            dma((4, 2)),
            dma((4, 2)),
            dma((4,)),
            dma((4,)),
            dma((2, 4, 2)),
            pltpu.VMEM((1, D), F32),
            pltpu.VMEM((8, PART), F32),
            dma((16,)),
            dma((16,)),
            dma((2, 4, 2)),
            dma((2, 4, 2)),
            dma((2, 4)),
            dma((2, 4)),
            dma((2, 2)),
            dma((2, 2)),
            dma((2, 2)),
            dma((2, 2)),
            dma((2, 4)),
            dma((2, 4)),
            dma((2, 4, 2)),
            dma((2, 4, 2)),
            dma((2, 4)),
            dma((2, 4)),
        ],
        compiler_params=pltpu.CompilerParams(
            collective_id=0, has_side_effects=True, vmem_limit_bytes=64 * 2**20 - 2**16
        ),
        cost_estimate=pl.CostEstimate(
            flops=26 * 10**9, bytes_accessed=40 * 10**6, transcendentals=10**6
        ),
        name="experts",
    )(meta, gain, fwd_sent[0], bwd_sent[0], bwd_saved[0], pre, w_in[0], w_out[0])
    return (fwd_out[None], bwd_out[None], gain_grad)


def solution(mesh):
    placed = (
        P("pp", "ep", None),
        P("pp", "ep", None),
        P("pp", "ep", None),
        P("pp", "ep", None, None),
        P("pp", "ep", None),
        P("pp", "ep", None),
        P("pp", "ep", None),
        P("pp", "ep", None),
        P("pp", None),
        P("pp", "ep", None),
        P("pp", None, "ep"),
    )
    return jax.shard_map(
        on_device,
        mesh=mesh,
        in_specs=placed,
        out_specs=(P("pp", "ep", None), P("pp", "ep", None), P("pp", None)),
        check_vma=False,
    )
```

```python
import jax
import jax.numpy as jnp
from jax import lax
from jax.experimental import pallas as pl
from jax.experimental.pallas import tpu as pltpu
from jax.sharding import PartitionSpec as P

D = 7168
FF = 1024
CAP = 72
TOK = 128
SLICE = 1792
PART = 896
ROWS = 2 * CAP
TILE = 256
EPS = 1e-06
HALVES = ((0, 768), (768, 1024))
PIECES = ((0, 512), (512, 512), (1024, 512), (1536, 256))
F32 = jnp.float32
BF16 = jnp.bfloat16
MESH = pl.DeviceIdType.MESH


def kernel(
    meta,
    gain,
    fwd_sent,
    bwd_sent,
    saved,
    pre,
    w_in,
    w_out,
    fwd_out,
    bwd_out,
    gain_grad,
    ret_f,
    ret_b,
    local_gain,
    w1,
    w2,
    v_f,
    v_b,
    x_f,
    x_b,
    s_f,
    s_b,
    part,
    r1_f,
    r1_b,
    r2_f,
    r2_b,
    h_f,
    h_b,
    xr_f,
    xr_b,
    pre_in,
    pre_out,
    pre_got,
    stage,
    meta_got,
    inv_out,
    inv_got,
    pick_f,
    pick_b,
    pick_pre,
    comb_f,
    comb_b,
    load_sem,
    stage_sem,
    out_sem,
    misc_send,
    misc_recv,
    pre_send,
    pre_recv,
    relay,
    near_send,
    far_send,
    relay_send,
    relay_recv,
    s1_recv,
    gain_got,
    gain_sum,
    gain_send,
    gain_recv,
    d_send,
    d_recv,
    r1_send,
    r1_recv,
    r2_send,
    r2_recv,
    ag_send,
    ag_recv,
    ac_send,
    ac_recv,
    ret_send,
    ret_recv,
    x_send,
    x_recv,
):
    p = lax.axis_index("pp")
    ep = lax.axis_index("ep")
    xh = ep // 8
    z = (ep // 2) % 4
    c = ep % 2
    zp = z % 2
    own_row = pl.multiple_of(xh * TOK, TOK)
    other_row = pl.multiple_of((1 - xh) * TOK, TOK)

    def place(section, dx, dz, dc):
        x2 = (xh + dx) % 2
        z2 = (z + dz) % 4
        c2 = (c + dc) % 2
        return {"pp": section, "ep": x2 * 8 + z2 * 2 + c2}

    def remote(src, dst, send, recv, target):
        return pltpu.make_async_remote_copy(
            src_ref=src,
            dst_ref=dst,
            send_sem=send,
            recv_sem=recv,
            device_id=target,
            device_id_type=MESH,
        )

    def columns(dz, dc):
        j = 2 * ((z + dz) % 2) + (c + dc) % 2
        return pl.multiple_of(j * SLICE, TILE)

    pairs = [(dz, dc, k) for dz, dc in ((0, 1), (0, 0), (1, 0), (1, 1)) for k in range(2)]
    near_z = 1 + 2 * zp
    far_z = 3 - 2 * zp
    mirror = 7 - 2 * z
    even = p % 2 == 0
    near = p + 1 - 2 * (p % 2)
    ahead = (p + 6 + 4 * (p % 2)) % 8

    loads = []
    for q in range(4):
        loads.append(
            pltpu.make_async_copy(
                fwd_sent.at[:, pl.ds(q * SLICE, SLICE)], s_f.at[q, pl.ds(0, TOK)], load_sem.at[q]
            )
        )
    loads.append(pltpu.make_async_copy(pre, pre_in, load_sem.at[4]))
    loads.append(pltpu.make_async_copy(w_in, w1, load_sem.at[5]))
    loads.append(pltpu.make_async_copy(w_out, w2, load_sem.at[6]))
    for load in loads:
        load.start()

    peers = [(near, 0, 0, 0), (near, 1, 0, 0), (7 - p, 0, 0, 0), (7 - p, 1, 0, 0)]
    peers += [((p + 2) % 8, 0, 0, 0), ((p + 6) % 8, 0, 0, 0), (p, 1, 0, 0), (p, 1, mirror, 0)]
    far = (p + 7 + 2 * (p % 2)) % 8
    peers += [(far, 0, 0, 0), (far, 1, 0, 0)]
    peers += [(p, 0, dz, dc) for dz in range(4) for dc in range(2) if (dz, dc) != (0, 0)]
    barrier = pltpu.get_barrier_semaphore()
    for peer in peers:
        pl.semaphore_signal(barrier, inc=1, device_id=place(*peer), device_id_type=MESH)
    pl.semaphore_wait(barrier, len(peers))

    meta_copy = remote(meta, meta_got, misc_send.at[0], misc_recv.at[0], place(p, 1, 0, 0))
    meta_copy.start()

    def half_columns(dz, dc, k):
        begin, size = HALVES[k]
        return pl.ds(pl.multiple_of(columns(dz, dc) + begin, TILE), size)

    def block_copies(src, dst, send, recv, dz, dc, k, stream):
        cols = half_columns(dz, dc, k)
        jr = 4 * dz + 2 * dc + k
        return [
            remote(
                src.at[:, cols],
                dst.at[pl.ds(own_row, TOK), cols],
                send.at[jr, dx],
                recv.at[stream, jr, dx],
                place(near, dx, 0, 0),
            )
            for dx in range(2)
        ]

    def relay_copy(src, dz, dc, k):
        cols = half_columns(dz, dc, k)
        jr = 4 * dz + 2 * dc + k
        return remote(
            src.at[:, cols],
            relay.at[:, cols],
            relay_send.at[jr],
            relay_recv.at[jr],
            place(ahead, 0, 0, 0),
        )

    def start_forward(pair):
        @pl.when(even)
        def _():
            for copy in block_copies(fwd_sent, v_f, near_send, s1_recv, *pair, 0):
                copy.start()

        @pl.when(jnp.logical_not(even))
        def _():
            relay_copy(fwd_sent, *pair).start()

    def relay_forward(pair):
        @pl.when(jnp.logical_not(even))
        def _():
            relay_copy(fwd_sent, *pair).wait_recv()
            for copy in block_copies(relay, v_f, far_send, s1_recv, *pair, 0):
                copy.start()

    def start_backward(pair):
        @pl.when(even)
        def _():
            relay_copy(bwd_sent, *pair).start()

    def relay_backward(pair):
        @pl.when(even)
        def _():
            relay_copy(bwd_sent, *pair).wait_recv()
            for copy in block_copies(relay, v_b, far_send, s1_recv, *pair, 1):
                copy.start()

        @pl.when(jnp.logical_not(even))
        def _():
            for copy in block_copies(bwd_sent, v_b, near_send, s1_recv, *pair, 1):
                copy.start()

    def arrived(stream, v, pair):
        for copy in block_copies(fwd_sent, v, near_send, s1_recv, *pair, stream):
            copy.wait_recv()

    for pair in pairs[:2]:
        start_forward(pair)

    own_meta = meta[...]
    row_id = lax.broadcasted_iota(jnp.int32, (TOK, TOK), 0)
    col_id = lax.broadcasted_iota(jnp.int32, (TOK, TOK), 1)
    before = jnp.where(row_id < col_id, 1.0, 0.0).astype(BF16)

    def slots(block, stream, expert):
        expert = expert.astype(F32)
        hit0 = jnp.where(block[2 * stream : 2 * stream + 1] == expert, 1.0, 0.0)
        hit1 = jnp.where(block[2 * stream + 1 : 2 * stream + 2] == expert, 1.0, 0.0)
        hit = hit0 + hit1
        wide = jnp.broadcast_to(hit, (16, TOK)).astype(BF16)
        slot = jnp.dot(wide, before, preferred_element_type=F32)[0:1]
        gate = (
            block[4 + 2 * stream : 5 + 2 * stream] * hit0
            + block[5 + 2 * stream : 6 + 2 * stream] * hit1
        )
        return hit0, hit1, hit, slot, gate

    loads[4].wait()
    pre_copies = {}
    for dx in range(2):
        for i in range(2):
            owner = z if i == 0 else 3 - z
            expert = 2 * ((xh + dx) % 2) + owner // 2
            hit0, hit1, _, slot, _ = slots(own_meta, 1, expert)
            hit_row = jnp.concatenate([hit0, hit1], axis=1)
            slot_row = jnp.concatenate([slot, slot], axis=1)
            line = lax.broadcasted_iota(jnp.int32, (80, 2 * TOK), 0).astype(F32)
            pick_pre[...] = jnp.where((line == slot_row) & (hit_row > 0.5), 1.0, 0.0).astype(BF16)
            target = pre_got.at[i, xh] if (dx, i) == (0, 0) else pre_out.at[2 * dx + i]

            def gather_pre(t, carry, target=target):
                cols = pl.ds(pl.multiple_of(t * 512, 512), 512)
                target[:, cols] = jnp.dot(
                    pick_pre[...], pre_in[:, cols], preferred_element_type=F32
                ).astype(BF16)
                return carry

            lax.fori_loop(0, 4, gather_pre, 0)
            if (dx, i) != (0, 0):
                copy = remote(
                    pre_out.at[2 * dx + i],
                    pre_got.at[i, xh],
                    pre_send.at[i, dx],
                    pre_recv.at[i, dx],
                    place(p, dx, i * mirror, 0),
                )
                copy.start()
                pre_copies[dx, i] = copy

    total = jnp.zeros((TOK, 1), F32)
    for q in range(4):
        loads[q].wait()
        block = s_f[q, pl.ds(0, TOK), :].astype(F32)
        total = total + jnp.sum(block * block, axis=1, keepdims=True)
    inv_out[...] = jnp.broadcast_to(lax.rsqrt(total / D + EPS), (TOK, 128))
    inv_copies = [
        remote(
            inv_out,
            inv_got.at[pl.ds(own_row, TOK)],
            misc_send.at[1 + dx],
            misc_recv.at[1 + dx],
            place((p + 1) % 8, dx, 0, 0),
        )
        for dx in range(2)
    ]
    for copy in inv_copies:
        copy.start()

    meta_copy.wait_recv()
    got_meta = meta_got[...]
    for stream, pick, comb in ((0, pick_f, comb_f), (1, pick_b, comb_b)):
        rows_needed = []
        for local in range(2):
            expert = 2 * xh + local
            own = slots(own_meta, stream, expert)
            got = slots(got_meta, stream, expert)
            low = xh == 0
            hit_row = jnp.concatenate(
                [jnp.where(low, own[2], got[2]), jnp.where(low, got[2], own[2])], axis=1
            )
            slot_row = jnp.concatenate(
                [jnp.where(low, own[3], got[3]), jnp.where(low, got[3], own[3]) + CAP], axis=1
            )
            line = lax.broadcasted_iota(jnp.int32, (ROWS, 2 * TOK), 0).astype(F32)
            pick[local] = jnp.where((line == slot_row) & (hit_row > 0.5), 1.0, 0.0).astype(BF16)
            for side in (own, got):
                rows_needed += [side[3], side[4]]
        padding = jnp.zeros((TOK - len(rows_needed), TOK), F32)
        turned = jnp.concatenate(rows_needed + [padding], axis=0).T
        lane = lax.broadcasted_iota(jnp.int32, (TOK, 2 * ROWS), 1).astype(F32)
        for side in range(2):
            home = jnp.where(xh == 0, side, 1 - side).astype(F32)
            mix = jnp.zeros((TOK, 2 * ROWS), F32)
            for local in range(2):
                k = 2 * (2 * local + side)
                slot_col = turned[:, k : k + 1] + (home * CAP + local * ROWS)
                gate_col = turned[:, k + 1 : k + 2]
                mix = mix + jnp.where(lane == slot_col, gate_col, 0.0)
            high = mix.astype(BF16)
            comb[pl.ds(2 * side * TOK, TOK), :] = high
            comb[pl.ds((2 * side + 1) * TOK, TOK), :] = (mix - high.astype(F32)).astype(BF16)

    rows0, rows1 = pl.ds(0, ROWS), pl.ds(ROWS, ROWS)
    partner = {"pp": p, "ep": xh * 8 + (z + 1 - 2 * zp) * 2 + c}
    fwd = dict(
        v=v_f, x=x_f, s=s_f, h=h_f, r1=r1_f, r2=r2_f, ret=ret_f, xr=xr_f, pick=pick_f, comb=comb_f
    )
    bwd = dict(
        v=v_b, x=x_b, s=s_b, h=h_b, r1=r1_b, r2=r2_b, ret=ret_b, xr=xr_b, pick=pick_b, comb=comb_b
    )
    fwd.update(number=0, width=2 * FF)
    bwd.update(number=1, width=FF)
    def dispatch(stream, dzp, dc, k):
        number, v, s, x = stream["number"], stream["v"], stream["s"], stream["x"]
        begin, size = HALVES[k]
        base = columns(dzp, dc) + begin
        targets = []
        for dz in (dzp, dzp + 2):
            here = x if (dz, dc) == (0, 0) else s
            targets.append((here, dz, ((z + dz) % 4) // 2))

        def gather(t, carry):
            cols = pl.ds(pl.multiple_of(base + t * TILE, TILE), TILE)
            block = v[:, cols]
            if number == 0:
                block = (block.astype(F32) * inv_got[:, 0:1] * gain[:, cols]).astype(BF16)
            where = pl.ds(pl.multiple_of(begin + t * TILE, TILE), TILE)
            for ref, dz, local in targets:
                ref[dz, pl.ds(dc * ROWS, ROWS), where] = jnp.dot(
                    stream["pick"][local], block, preferred_element_type=F32
                ).astype(BF16)
            return carry

        lax.fori_loop(0, size // TILE, gather, 0)
        for dz in (dzp + 2, dzp):
            if (dz, dc) != (0, 0):
                moved(stream, dz, dc, k).start()

    def multiply(lhs, w, out, count, tile, turned):
        def step(t, carry):
            cols = pl.ds(pl.multiple_of(t * tile, tile), tile)
            if turned:
                got = lax.dot_general(
                    lhs[...], w[cols, :], (((1,), (1,)), ((), ())), preferred_element_type=F32
                )
            else:
                got = jnp.dot(lhs[...], w[:, cols], preferred_element_type=F32)
            out[:, cols] = got.astype(BF16)
            return carry

        lax.fori_loop(0, count // tile, step, 0)

    def moved(stream, dz, dc, k):
        rows, cols = pl.ds(dc * ROWS, ROWS), pl.ds(*HALVES[k])
        number = stream["number"]
        return remote(
            stream["s"].at[dz, rows, cols],
            stream["x"].at[dz, rows, cols],
            d_send.at[number, dz, dc, k],
            d_recv.at[number, dz, dc, k],
            place(p, 0, dz, dc),
        )

    def to_other_core(stream, dz):
        number, width = stream["number"], stream["width"]
        return remote(
            part.at[dz, rows1, pl.ds(0, width)],
            stream["r1"].at[dz],
            r1_send.at[number, dz],
            r1_recv.at[number, dz],
            place(p, 0, 0, 1),
        )

    def first_product(stream, slot):
        number, x, width = stream["number"], stream["x"], stream["width"]
        dz = slot_dz[slot]
        for dc in range(2):
            if (slot, dc) != ("own", 0):
                for k in range(2):
                    moved(stream, dz, dc, k).wait_recv()
        if number == 1:
            to_other_core(fwd, dz).wait_send()
            if slot in passed_on:
                to_partner(fwd, slot).wait_send()
        out = part.at[dz, :, pl.ds(0, width)]
        if number == 0:
            multiply(x.at[dz], w1, out, width, 512, False)
        else:
            multiply(x.at[dz], w2, out, width, 512, True)
        to_other_core(stream, dz).start()

    slot_dz = {"own": 0, "near": near_z, "two": 2, "far": far_z}
    passed_on = {"far": 0, "two": 1}

    def to_partner(stream, slot):
        number, width = stream["number"], stream["width"]
        i = passed_on[slot]
        return remote(
            part.at[slot_dz[slot], rows0, pl.ds(0, width)],
            stream["r2"].at[i],
            r2_send.at[number, i],
            r2_recv.at[number, i],
            partner,
        )

    def chip_sum(stream, slot):
        r1, width = stream["r1"], stream["width"]
        dz = slot_dz[slot]
        to_other_core(stream, dz).wait_recv()

        def add(t, carry):
            cols = pl.ds(pl.multiple_of(t * 512, 512), 512)
            part[dz, rows0, cols] = (
                part[dz, rows0, cols].astype(F32) + r1[dz, :, cols].astype(F32)
            ).astype(BF16)
            return carry

        lax.fori_loop(0, width // 512, add, 0)
        if slot in passed_on:
            to_partner(stream, slot).start()

    def share_core(stream, slot):
        number, h, dz = stream["number"], stream["h"], slot_dz[slot]
        return remote(
            h.at[dz, rows0],
            h.at[dz, rows1],
            ac_send.at[number, dz],
            ac_recv.at[number, dz],
            place(p, 0, 0, 1),
        )

    def share_partner(stream, i):
        number, h = stream["number"], stream["h"]
        there = 3 - 2 * (1 - zp) if i == 0 else 2
        return remote(
            h.at[0 if i == 0 else near_z, rows0],
            h.at[there, rows0],
            ag_send.at[number, i],
            ag_recv.at[number, i],
            partner,
        )

    def activate(stream, slot):
        number, h, r2 = stream["number"], stream["h"], stream["r2"]
        i = 0 if slot == "own" else 1
        dz = slot_dz[slot]
        to_partner(stream, "far" if i == 0 else "two").wait_recv()
        if number == 1:
            for dx in range(2):
                if (dx, i) != (0, 0):
                    pre_copies[dx, i].wait_recv()

        def step(t, carry):
            lo = pl.ds(pl.multiple_of(t * TILE, TILE), TILE)
            hi = pl.ds(pl.multiple_of(t * TILE + FF, TILE), TILE)
            if number == 0:
                g = part[dz, rows0, lo].astype(F32) + r2[i, :, lo].astype(F32)
                u = part[dz, rows0, hi].astype(F32) + r2[i, :, hi].astype(F32)
                h[dz, rows0, lo] = (g / (1.0 + jnp.exp(-g)) * u).astype(BF16)
            else:
                hg = part[dz, rows0, lo].astype(F32) + r2[i, :, lo].astype(F32)
                g = jnp.concatenate(
                    [pre_got[i, k, :, lo].astype(F32)[0:CAP] for k in range(2)], axis=0
                )
                u = jnp.concatenate(
                    [pre_got[i, k, :, hi].astype(F32)[0:CAP] for k in range(2)], axis=0
                )
                sig = 1.0 / (1.0 + jnp.exp(-g))
                h[dz, rows0, lo] = (hg * u * sig * (1.0 + g * (1.0 - sig))).astype(BF16)
                h[dz, rows0, hi] = (hg * g * sig).astype(BF16)
            return carry

        lax.fori_loop(0, FF // TILE, step, 0)
        share_partner(stream, i).start()
        share_core(stream, slot).start()

    def forward_on(stream, slot):
        share_partner(stream, passed_on[slot]).wait_recv()
        share_core(stream, slot).start()

    def back(stream, dz, dc, n):
        number, s = stream["number"], stream["s"]
        begin, size = PIECES[n]
        region = stream["ret"].at[
            pl.ds(pl.multiple_of(z // 2 * ROWS, ROWS), ROWS),
            pl.ds(pl.multiple_of(columns(0, 0) + begin, TILE), size),
        ]
        source = s.at[dz, pl.ds(dc * ROWS, ROWS), pl.ds(begin, size)]
        if isinstance(dz, int) and (dz, dc) == (0, 0):
            return pltpu.make_async_copy(source, region, ret_recv.at[number, 0, 0, n])
        return remote(
            source,
            region,
            ret_send.at[number, dz, dc, n],
            ret_recv.at[number, dz, dc, n],
            place(p, 0, 4 - dz, dc),
        )

    def second_product(stream, slot, n):
        number, h, s = stream["number"], stream["h"], stream["s"]
        dz = slot_dz[slot]
        begin, size = PIECES[n]
        if n == 0:
            share_core(stream, slot).wait_recv()
            for dc in range(2):
                if (slot, dc) != ("own", 0):
                    for k in range(2):
                        moved(stream, dz, dc, k).wait_send()
        out = s.at[dz, :, pl.ds(begin, size)]
        if number == 0:
            multiply(h.at[dz], w2.at[:, pl.ds(begin, size)], out, size, TILE, False)
        else:
            multiply(h.at[dz], w1.at[pl.ds(begin, size)], out, size, TILE, True)
        for dc in (1, 0):
            back(stream, dz, dc, n).start()

    def cross(stream, dzp, dc, n):
        number, v = stream["number"], stream["v"]
        begin, size = PIECES[n]
        cols = pl.ds(pl.multiple_of(columns(dzp, dc) + begin, TILE), size)
        return remote(
            v.at[pl.ds(other_row, TOK), cols],
            stream["xr"].at[:, cols],
            x_send.at[number, n, 2 * dzp + dc],
            x_recv.at[number, n, 2 * dzp + dc],
            place(p, 1, 0, 0),
        )

    def combine(stream, n):
        v, x, ret = stream["v"], stream["x"], stream["ret"]
        begin, size = PIECES[n]
        fetches = []
        for dzp, dc in late:
            for dz in (dzp, dzp + 2):
                if (dz, dc) == (0, 0):
                    back(stream, dz, dc, n).wait()
                else:
                    back(stream, dz, dc, n).wait_recv()
            jr = 2 * dzp + dc
            cols = pl.ds(pl.multiple_of(columns(dzp, dc) + begin, TILE), size)
            fetch = pltpu.make_async_copy(
                ret.at[:, cols], stage.at[jr, :, pl.ds(0, size)], stage_sem.at[jr]
            )
            fetch.start()
            fetches.append(fetch)
        for fetch, (dzp, dc) in zip(fetches, late):
            fetch.wait()
            base = columns(dzp, dc) + begin
            jr = 2 * dzp + dc

            def step(t, carry, base=base, jr=jr):
                cols = pl.ds(pl.multiple_of(t * TILE, TILE), TILE)
                mixed = jnp.dot(
                    stream["comb"][...], stage[jr, :, cols], preferred_element_type=F32
                )
                own = mixed[0:TOK] + mixed[TOK : 2 * TOK]
                other = mixed[2 * TOK : 3 * TOK] + mixed[3 * TOK :]
                high = own.astype(BF16)
                kept = pl.ds(pl.multiple_of(begin + t * TILE, TILE), TILE)
                x[jr, pl.ds(0, TOK), kept] = high
                x[jr, pl.ds(TOK, TOK), kept] = (own - high.astype(F32)).astype(BF16)
                out_cols = pl.ds(pl.multiple_of(base + t * TILE, TILE), TILE)
                v[pl.ds(other_row, TOK), out_cols] = other.astype(BF16)
                return carry

            lax.fori_loop(0, size // TILE, step, 0)
            cross(stream, dzp, dc, n).start()

    late = [(0, 1), (0, 0), (1, 1), (1, 0)]

    def finish_forward(n):
        begin, size = PIECES[n]
        for dzp, dc in late:
            cross(fwd, dzp, dc, n).wait_recv()
            base = columns(dzp, dc)
            jr = 2 * dzp + dc

            def step(t, carry, base=base, jr=jr):
                cols = pl.ds(pl.multiple_of(begin + t * TILE, TILE), TILE)
                wide = pl.ds(pl.multiple_of(base + begin + t * TILE, TILE), TILE)
                here = pl.ds(own_row, TOK)
                mine = x_f[jr, pl.ds(0, TOK), cols].astype(F32)
                mine = mine + x_f[jr, pl.ds(TOK, TOK), cols].astype(F32)
                v_f[here, wide] = (
                    v_f[here, wide].astype(F32) + (mine + xr_f[:, wide].astype(F32))
                ).astype(BF16)
                return carry

            lax.fori_loop(0, size // TILE, step, 0)

    def write_forward():
        copy = pltpu.make_async_copy(v_f.at[pl.ds(own_row, TOK)], fwd_out, out_sem.at[0, 0])
        copy.start()
        outs.append(copy)

    def backward_start():
        total = jnp.zeros((TOK, 1), F32)
        for n, (dzp, dc) in enumerate(late):
            saved_loads[n].wait()
            block = s_f[2 * dzp + dc, pl.ds(0, TOK), :].astype(F32)
            total = total + jnp.sum(block * block, axis=1, keepdims=True)
        return lax.rsqrt(total / D + EPS)

    def backward_piece(n, inv, dots):
        begin, size = PIECES[n]
        for dzp, dc in late:
            cross(bwd, dzp, dc, n).wait_recv()
            base = columns(dzp, dc)
            jr = 2 * dzp + dc

            def step(t, carry, base=base, jr=jr):
                cols = pl.ds(pl.multiple_of(begin + t * TILE, TILE), TILE)
                wide = pl.ds(pl.multiple_of(base + begin + t * TILE, TILE), TILE)
                grad = x_b[jr, pl.ds(0, TOK), cols].astype(F32)
                grad = grad + x_b[jr, pl.ds(TOK, TOK), cols].astype(F32)
                grad = grad + xr_b[:, wide].astype(F32)
                high = grad.astype(BF16)
                x_b[jr, pl.ds(0, TOK), cols] = high
                x_b[jr, pl.ds(TOK, TOK), cols] = (grad - high.astype(F32)).astype(BF16)
                w = s_f[jr, pl.ds(0, TOK), cols].astype(F32)
                local_gain[:, wide] = jnp.sum(grad * w * inv, axis=0, keepdims=True)
                return carry + w * gain[:, wide] * grad

            dots = lax.fori_loop(0, size // TILE, step, dots)
        return dots

    def finish_backward(inv, dots):
        scale = inv * inv * inv * (jnp.sum(dots, axis=1, keepdims=True) / D)
        waiting = gain_cores()
        for n, (dzp, dc) in enumerate(late):
            if n == 1:
                waiting = gain_sides(waiting)
            if n == 2:
                waiting = gain_spread(waiting)
            base = columns(dzp, dc)
            jr = 2 * dzp + dc

            def last(t, carry, base=base, jr=jr):
                cols = pl.ds(pl.multiple_of(t * TILE, TILE), TILE)
                wide = pl.ds(pl.multiple_of(base + t * TILE, TILE), TILE)
                here = pl.ds(own_row, TOK)
                grad = x_b[jr, pl.ds(0, TOK), cols].astype(F32)
                grad = grad + x_b[jr, pl.ds(TOK, TOK), cols].astype(F32)
                w = s_f[jr, pl.ds(0, TOK), cols].astype(F32)
                v_b[here, wide] = (
                    v_b[here, wide].astype(F32) + inv * (gain[:, wide] * grad) - w * scale
                ).astype(BF16)
                return carry

            lax.fori_loop(0, SLICE // TILE, last, 0)
            copy = pltpu.make_async_copy(
                v_b.at[pl.ds(own_row, TOK), pl.ds(base, SLICE)],
                bwd_out.at[:, pl.ds(base, SLICE)],
                out_sem.at[1, jr],
            )
            copy.start()
            outs.append(copy)
        for copy in waiting:
            copy.wait_recv()

    half = pl.multiple_of(c * 4 * PART, 128)
    half_other = pl.multiple_of((1 - c) * 4 * PART, 128)
    gain_copies = []

    def send_gain(src, dst, index, target):
        copy = remote(src, dst, gain_send.at[index], gain_recv.at[index], target)
        copy.start()
        gain_copies.append(copy)
        return copy

    def piece(dz):
        return pl.ds(pl.multiple_of(half + (z + dz) % 4 * PART, 128), PART)

    def gain_cores():
        size = pl.ds(half_other, 4 * PART)
        copy = send_gain(local_gain.at[:, size], gain_got.at[:, size], 0, place(p, 0, 0, 1))
        copy.wait_recv()
        size = pl.ds(half, 4 * PART)
        local_gain[:, size] = local_gain[:, size] + gain_got[:, size]
        return [
            send_gain(
                local_gain.at[:, piece(dz)], gain_sum.at[pl.ds(dz, 1)], dz, place(p, 0, dz, 0)
            )
            for dz in range(1, 4)
        ]

    def gain_sides(copies):
        for copy in copies:
            copy.wait_recv()
        mine = local_gain[:, piece(0)]
        for dz in range(1, 4):
            mine = mine + gain_sum[pl.ds(dz, 1)]
        gain_sum[0:1] = mine
        targets = [place(p, 1, 0, 0), place(7 - p, 0, 0, 0), place(7 - p, 1, 0, 0)]
        return [
            send_gain(gain_sum.at[pl.ds(0, 1)], gain_sum.at[pl.ds(4 + i, 1)], 4 + i, target)
            for i, target in enumerate(targets)
        ]

    def gain_spread(copies):
        for copy in copies:
            copy.wait_recv()
        here = gain_sum[0:1] + gain_sum[4:5]
        gain_grad[:, piece(0)] = here + (gain_sum[5:6] + gain_sum[6:7])
        return [
            send_gain(
                gain_grad.at[:, piece(0)],
                gain_grad.at[:, piece(0)],
                8 + 2 * dz + dc,
                place(p, 0, dz, dc),
            )
            for dz in range(4)
            for dc in range(2)
            if (dz, dc) != (0, 0)
        ]

    def sends_done(copies):
        for copy in copies:
            copy.wait_send()

    outs = []
    for copy in inv_copies:
        copy.wait_recv()

    def dispatch_forward(n):
        for i in (2 * n, 2 * n + 1):
            relay_forward(pairs[i])
            start_backward(pairs[i])
            arrived(0, v_f, pairs[i])
            if i < 6:
                start_forward(pairs[i + 2])
            dispatch(fwd, *pairs[i])

    def dispatch_backward(n):
        for i in (2 * n, 2 * n + 1):
            arrived(1, v_b, pairs[i])
            if i + 3 < 8:
                relay_backward(pairs[i + 3])
            dispatch(bwd, *pairs[i])

    dispatch_forward(0)
    dispatch_forward(1)
    dispatch_forward(2)
    loads[5].wait()
    first_product(fwd, "two")
    dispatch_forward(3)
    chip_sum(fwd, "two")
    for pair in pairs[:3]:
        relay_backward(pair)
    first_product(fwd, "far")
    first_product(fwd, "own")
    chip_sum(fwd, "far")
    first_product(fwd, "near")
    chip_sum(fwd, "own")
    chip_sum(fwd, "near")
    loads[6].wait()
    dispatch_backward(0)
    dispatch_backward(1)
    activate(fwd, "near")
    activate(fwd, "own")
    dispatch_backward(2)
    dispatch_backward(3)
    for n in (0, 1):
        second_product(fwd, "own", n)
        second_product(fwd, "near", n)
    first_product(bwd, "two")
    chip_sum(bwd, "two")
    forward_on(fwd, "two")
    forward_on(fwd, "far")
    for n in (0, 1):
        second_product(fwd, "two", n)
        second_product(fwd, "far", n)
    first_product(bwd, "far")
    chip_sum(bwd, "far")
    for n in (2, 3):
        for slot in ("two", "far", "own", "near"):
            second_product(fwd, slot, n)
    first_product(bwd, "own")
    first_product(bwd, "near")
    chip_sum(bwd, "own")
    chip_sum(bwd, "near")
    combine(fwd, 0)
    activate(bwd, "near")
    activate(bwd, "own")
    combine(fwd, 1)
    for n in (0, 1):
        second_product(bwd, "own", n)
        second_product(bwd, "near", n)
    combine(fwd, 2)
    combine(fwd, 3)
    forward_on(bwd, "two")
    forward_on(bwd, "far")
    for n in (0, 1):
        second_product(bwd, "two", n)
        second_product(bwd, "far", n)
    for n in (2, 3):
        for slot in ("two", "far", "own", "near"):
            second_product(bwd, slot, n)
    for n in range(4):
        for dz in range(4):
            for dc in range(2):
                if (dz, dc) != (0, 0):
                    back(fwd, dz, dc, n).wait_send()
    saved_loads = []
    for n, (dzp, dc) in enumerate(late):
        copy = pltpu.make_async_copy(
            saved.at[:, pl.ds(columns(dzp, dc), SLICE)],
            s_f.at[2 * dzp + dc, pl.ds(0, TOK)],
            load_sem.at[n],
        )
        copy.start()
        saved_loads.append(copy)
    for n in range(4):
        finish_forward(n)
    write_forward()
    inv = backward_start()
    dots = jnp.zeros((TOK, TILE), F32)
    combine(bwd, 0)
    combine(bwd, 1)
    dots = backward_piece(0, inv, dots)
    combine(bwd, 2)
    dots = backward_piece(1, inv, dots)
    combine(bwd, 3)
    dots = backward_piece(2, inv, dots)
    dots = backward_piece(3, inv, dots)
    finish_backward(inv, dots)

    sends_done([meta_copy] + inv_copies + list(pre_copies.values()) + gain_copies)
    for pair in pairs:
        relay_copy(fwd_sent, *pair).wait_send()
        for copy in block_copies(fwd_sent, v_f, near_send, s1_recv, *pair, 0):
            copy.wait_send()
        for copy in block_copies(relay, v_f, far_send, s1_recv, *pair, 0):
            copy.wait_send()
    for stream in (fwd, bwd):
        for slot in slot_dz:
            share_core(stream, slot).wait_send()
        for i in range(2):
            share_partner(stream, i).wait_send()
        for n in range(4):
            for dzp, dc in late:
                cross(stream, dzp, dc, n).wait_send()
    for slot in slot_dz:
        to_other_core(bwd, slot_dz[slot]).wait_send()
    for slot in passed_on:
        to_partner(bwd, slot).wait_send()
    for n in range(4):
        for dz in range(4):
            for dc in range(2):
                if (dz, dc) != (0, 0):
                    back(bwd, dz, dc, n).wait_send()
    for copy in outs:
        copy.wait()


def on_device(
    fwd_sent,
    bwd_sent,
    bwd_saved,
    bwd_pre,
    fwd_route,
    bwd_route,
    fwd_gate,
    bwd_gate,
    gain,
    w_in,
    w_out,
):
    meta = jnp.concatenate(
        [
            fwd_route[0].T.astype(F32),
            bwd_route[0].T.astype(F32),
            fwd_gate[0].T,
            bwd_gate[0].T,
        ],
        axis=0,
    )
    pre = jnp.transpose(bwd_pre[0], (1, 0, 2)).reshape(2 * TOK, 2 * FF)
    anywhere = pl.BlockSpec(memory_space=pl.ANY)
    vmem = pl.BlockSpec(memory_space=pltpu.VMEM)
    dma = pltpu.SemaphoreType.DMA

    def buf(*shape):
        return pltpu.VMEM(shape, BF16)

    fwd_out, bwd_out, gain_grad, _, _ = pl.pallas_call(
        kernel,
        out_shape=(
            jax.ShapeDtypeStruct((TOK, D), BF16),
            jax.ShapeDtypeStruct((TOK, D), BF16),
            jax.ShapeDtypeStruct((1, D), F32),
            jax.ShapeDtypeStruct((2 * ROWS, D), BF16),
            jax.ShapeDtypeStruct((2 * ROWS, D), BF16),
        ),
        in_specs=[vmem, vmem] + [anywhere] * 6,
        out_specs=(anywhere, anywhere, vmem, anywhere, anywhere),
        scratch_shapes=[
            pltpu.VMEM((1, D), F32),
            buf(SLICE, 2 * FF),
            buf(FF, SLICE),
            buf(2 * TOK, D),
            buf(2 * TOK, D),
            buf(4, 2 * ROWS, SLICE),
            buf(4, 2 * ROWS, SLICE),
            buf(4, 2 * ROWS, SLICE),
            buf(4, 2 * ROWS, SLICE),
            buf(4, 2 * ROWS, 2 * FF),
            buf(4, ROWS, 2 * FF),
            buf(4, ROWS, FF),
            buf(2, ROWS, 2 * FF),
            buf(2, ROWS, FF),
            buf(4, 2 * ROWS, FF),
            buf(4, 2 * ROWS, 2 * FF),
            buf(TOK, D),
            buf(TOK, D),
            buf(2 * TOK, 2 * FF),
            buf(4, 80, 2 * FF),
            buf(2, 2, 80, 2 * FF),
            buf(4, 2 * ROWS, 512),
            pltpu.VMEM((8, TOK), F32),
            pltpu.VMEM((TOK, 128), F32),
            pltpu.VMEM((2 * TOK, 128), F32),
            buf(2, ROWS, 2 * TOK),
            buf(2, ROWS, 2 * TOK),
            buf(80, 2 * TOK),
            buf(4 * TOK, 2 * ROWS),
            buf(4 * TOK, 2 * ROWS),
            dma((8,)),
            dma((4,)),
            dma((2, 4)),
            dma((4,)),
            dma((4,)),
            dma((2, 2)),
            dma((2, 2)),
            buf(TOK, D),
            dma((8, 2)),
            dma((8, 2)),
            dma((8,)),
            dma((8,)),
            dma((2, 8, 2)),
            pltpu.VMEM((1, D), F32),
            pltpu.VMEM((8, PART), F32),
            dma((16,)),
            dma((16,)),
            dma((2, 4, 2, 2)),
            dma((2, 4, 2, 2)),
            dma((2, 4)),
            dma((2, 4)),
            dma((2, 2)),
            dma((2, 2)),
            dma((2, 2)),
            dma((2, 2)),
            dma((2, 4)),
            dma((2, 4)),
            dma((2, 4, 2, 4)),
            dma((2, 4, 2, 4)),
            dma((2, 4, 4)),
            dma((2, 4, 4)),
        ],
        compiler_params=pltpu.CompilerParams(
            collective_id=0, has_side_effects=True, vmem_limit_bytes=64 * 2**20 - 2**16
        ),
        cost_estimate=pl.CostEstimate(
            flops=26 * 10**9, bytes_accessed=40 * 10**6, transcendentals=10**6
        ),
        name="experts",
    )(meta, gain, fwd_sent[0], bwd_sent[0], bwd_saved[0], pre, w_in[0], w_out[0])
    return (fwd_out[None], bwd_out[None], gain_grad)


def solution(mesh):
    placed = (
        P("pp", "ep", None),
        P("pp", "ep", None),
        P("pp", "ep", None),
        P("pp", "ep", None, None),
        P("pp", "ep", None),
        P("pp", "ep", None),
        P("pp", "ep", None),
        P("pp", "ep", None),
        P("pp", None),
        P("pp", "ep", None),
        P("pp", None, "ep"),
    )
    return jax.shard_map(
        on_device,
        mesh=mesh,
        in_specs=placed,
        out_specs=(P("pp", "ep", None), P("pp", "ep", None), P("pp", None)),
        check_vma=False,
    )
```
